256 devices in a mesh: liq: 4 (over x), ill: 8 (over y, core), dur: 8 (over z).
Axes of the slice: x: 4, y: 4, z: 8, core: 2. Of those that a mesh axis runs over, the one named last changes fastest.
Arguments:
- marginal_value: float32 [32, 16, 16, 512], P(None, 'dur', 'ill', 'liq'), may hold values from 0.5 to 2
- transition: float32 [32, 32], replicated, may hold values from 0 to 1, as said below
- discount_shock: float32 [32], replicated, may hold values from 0.5 to 2
- illiquid_drift: float32 [16], P('ill'), may hold values from 0.2 to 0.8
- durable_keep: float32 [16], P('dur'), may hold values from 0.3 to 0.9
- bracket_index: int32 [32, 16, 16, 512], P(None, 'dur', 'ill', 'liq'), may hold values from 0 to 510
- bracket_weight: float32 [32, 16, 16, 512], P(None, 'dur', 'ill', 'liq'), may hold values from 0 to 1
- steady_consumption: float32 [32, 16, 16, 512], P(None, 'dur', 'ill', 'liq'), may hold values from 0.8 to 1.6
- lottery_weight: float32 [32, 16, 16, 512], P(None, 'dur', 'ill', 'liq'), may hold values from 0 to 1
- liquid_target: int32 [32, 16, 16, 512], P(None, 'dur', 'ill', 'liq'), may hold values from 0 to 510
- illiquid_target: int32 [32, 16, 16], P(None, 'dur', 'ill'), may hold values from 0 to 15
- population: float32 [32, 16, 16, 512], P(None, 'dur', 'ill', 'liq'), may hold values from 0.5 to 2
Outputs:
- consumption: float32 [32, 16, 16, 512], P(None, 'dur', 'ill', 'liq')
- population_next: float32 [32, 16, 16, 512], P(None, 'dur', 'ill', 'liq')
The draws below stay inside these ranges and needn't reach their ends.
Inputs may be any that keep to these rules, and one draw needn't show every extreme that they name: `bracket_index`: global liquid index; the upper bracket point is index + 1. `liquid_target`: global liquid index; the upper target is index + 1. `illiquid_target`: global illiquid index. `transition`: entries positive, every row sums to one.
All inputs are finite; a program needn't handle non-finite values.
Results may differ from the reference program's by a relative error of at most 0.000065.
Values sent between devices are 32-bit elements; how exact they have to be, the bound alone decides.
No kernel may reach another device: no remote copies, remote signals or barrier semaphores. Data moves between devices by JAX's collectives and lax.ppermute only.
A program may use at most 64 MiB of HBM per device.

```python
import math
import jax
import jax.numpy as jnp
from jax import lax

Z = 32
NB = 512
NA = 16
ND = 16


def draw_transition(key, part):
    key_spread, key_diagonal = jax.random.split(key)
    spread = jax.random.uniform(key_spread, (Z, Z), jnp.float32, 0.2, 1.0)
    diagonal = jax.random.uniform(key_diagonal, (Z,), jnp.float32, 20.0, 30.0)
    raw_matrix = spread + jnp.diag(diagonal)
    return raw_matrix / jnp.sum(raw_matrix, axis=1, keepdims=True)


def place_ends(array, stream_key, low, top_value):
    extent = array.shape
    index_at = [jax.random.randint(jax.random.fold_in(stream_key, axis), (), 0, extent[axis]) for axis in range(len(extent))]
    array = array.at[tuple(index_at)].set(low)
    longest = extent.index(max(extent))
    index_at[longest] = (index_at[longest] + 1) % extent[longest]
    return array.at[tuple(index_at)].set(top_value)


def block_levels(stream_key, dims, pieces, least, high):
    level, own = 1.0, jax.random.fold_in(stream_key, 6)
    for position, shards_of in pieces:
        heights = jnp.exp(jax.random.uniform(jax.random.fold_in(own, position), (shards_of,), jnp.float32, least / len(pieces), high / len(pieces)))
        level = level * jnp.repeat(heights, dims[position] // shards_of).reshape([-1 if axis == position else 1 for axis in range(len(dims))])
    return level


def setup_inputs(seed: int = 0) -> dict:
    key_list = jax.random.split(jax.random.key(seed), 13)
    return {
        "marginal_value": jnp.clip(jnp.exp(math.log(2.0) - 1.3862944 * jax.random.uniform(key_list[0], (Z, ND, NA, NB), jnp.float32) ** block_levels(key_list[0], (Z, ND, NA, NB), ((1, 8), (2, 8), (3, 4)), -0.2, 0.2)), 0.5, 2.0),
        "transition": draw_transition(jax.random.fold_in(key_list[12], 71), 0),
        "discount_shock": jnp.clip(jnp.exp(jax.random.uniform(key_list[2], (Z,), jnp.float32, math.log(0.5), math.log(2.0))), 0.5, 2.0),
        "illiquid_drift": jnp.clip(0.2 + 0.6 * jax.random.uniform(key_list[3], (NA,), jnp.float32) ** block_levels(key_list[3], (NA,), ((0, 8),), -0.2, 0.2), 0.2, 0.8),
        "durable_keep": jnp.clip(0.3 + 0.59999996 * jax.random.uniform(key_list[4], (ND,), jnp.float32) ** block_levels(key_list[4], (ND,), ((0, 8),), -0.2, 0.2), 0.3, 0.9),
        "bracket_index": place_ends(jax.random.randint(key_list[5], (Z, ND, NA, NB), 0, NB - 1), jax.random.fold_in(key_list[5], 1), 0, (NB - 1) - 1).astype(jnp.int32),
        "bracket_weight": jnp.clip(1.0 * jax.random.uniform(key_list[6], (Z, ND, NA, NB), jnp.float32) ** block_levels(key_list[6], (Z, ND, NA, NB), ((1, 8), (2, 8), (3, 4)), -0.2, 0.2), 0.0, 1.0),
        "steady_consumption": jnp.clip(0.8 + 0.8 * jax.random.uniform(key_list[7], (Z, ND, NA, NB), jnp.float32) ** block_levels(key_list[7], (Z, ND, NA, NB), ((1, 8), (2, 8), (3, 4)), -0.2, 0.2), 0.8, 1.6),
        "lottery_weight": jnp.clip(1.0 * jax.random.uniform(key_list[8], (Z, ND, NA, NB), jnp.float32) ** block_levels(key_list[8], (Z, ND, NA, NB), ((1, 8), (2, 8), (3, 4)), -0.2, 0.2), 0.0, 1.0),
        "liquid_target": place_ends(jax.random.randint(key_list[9], (Z, ND, NA, NB), 0, NB - 1), jax.random.fold_in(key_list[9], 1), 0, (NB - 1) - 1).astype(jnp.int32),
        "illiquid_target": place_ends(jax.random.randint(key_list[10], (Z, ND, NA), 0, NA), jax.random.fold_in(key_list[10], 1), 0, NA - 1).astype(jnp.int32),
        "population": jnp.clip(jnp.exp(math.log(2.0) - 1.3862944 * jax.random.uniform(key_list[11], (Z, ND, NA, NB), jnp.float32) ** block_levels(key_list[11], (Z, ND, NA, NB), ((1, 8), (2, 8), (3, 4)), -0.2, 0.2)), 0.5, 2.0),
    }


DISCOUNT = 0.96
GROSS_RATE = 1.01
SLOPE_GAIN = 0.5
HIGHEST_PREC = lax.Precision.HIGHEST

def expect_upper(values, transition, drift_rate):
    expected = jnp.einsum('zy,ydab->zdab', transition, values, precision=HIGHEST_PREC)
    upper_plane = jnp.concatenate([expected[:, :, 1:, :], expected[:, :, -1:, :]], axis=2)
    drift_full = drift_rate[None, None, :, None]
    return drift_full * expected + (1.0 - drift_full) * upper_plane

def backward_step(values, transition, drift_rate, shock_scale, bracket_index, bracket_weight):
    drifted = expect_upper(values, transition, drift_rate)
    endogenous = lax.rsqrt(DISCOUNT * GROSS_RATE * shock_scale[:, None, None, None] * drifted)
    lower_value = jnp.take_along_axis(endogenous, bracket_index, axis=3)
    upper_value = jnp.take_along_axis(endogenous, bracket_index + 1, axis=3)
    return bracket_weight * lower_value + (1.0 - bracket_weight) * upper_value

def reference(marginal_value, transition, discount_shock, illiquid_drift, durable_keep, bracket_index, bracket_weight, steady_consumption, lottery_weight, liquid_target, illiquid_target, population):
    policy_one = backward_step(marginal_value, transition, illiquid_drift, discount_shock, bracket_index, bracket_weight)
    value_two = GROSS_RATE / (policy_one * policy_one)
    consumption = backward_step(value_two, transition, illiquid_drift, jnp.ones_like(discount_shock), bracket_index, bracket_weight)
    share = jnp.clip(lottery_weight + SLOPE_GAIN * (policy_one - steady_consumption), 0.0, 1.0)
    incomes, durables, ill_count, liq_count = population.shape
    inc_idx = lax.broadcasted_iota(jnp.int32, population.shape, 0)
    dur_idx = lax.broadcasted_iota(jnp.int32, population.shape, 1)
    ill_dest = jnp.broadcast_to(illiquid_target[:, :, :, None], population.shape).astype(jnp.int32)
    base_index = ((inc_idx * durables + dur_idx) * ill_count + ill_dest) * liq_count
    flat_mass = jnp.zeros((incomes * durables * ill_count * liq_count,), jnp.float32)
    flat_mass = flat_mass.at[(base_index + liquid_target).reshape(-1)].add((population * share).reshape(-1))
    flat_mass = flat_mass.at[(base_index + liquid_target + 1).reshape(-1)].add((population * (1.0 - share)).reshape(-1))
    lottery_mass = flat_mass.reshape(population.shape)
    dur_plane = lax.broadcasted_iota(jnp.int32, (durables,), 0)
    stay_share = jnp.where(dur_plane == 0, 1.0, durable_keep)[None, :, None, None]
    depart = (1.0 - stay_share) * lottery_mass
    settled = stay_share * lottery_mass + jnp.concatenate([depart[:, 1:], jnp.zeros_like(depart[:, :1])], axis=1)
    population_next = jnp.einsum('zy,zdab->ydab', transition, settled, precision=HIGHEST_PREC)
    return (consumption, population_next)
```

```python
import functools

import jax
import jax.numpy as jnp
from jax import lax
from jax.experimental import pallas as pl
from jax.experimental.pallas import tpu as pltpu
from jax.sharding import PartitionSpec as P

DISCOUNT = 0.96
GROSS_RATE = 1.01
SLOPE_GAIN = 0.5
HIGHEST_PREC = lax.Precision.HIGHEST

Z = 32
LANES = 128
PLANE_ROWS = 4 * Z
HALF_ROWS = 2 * Z
VMEM = pltpu.VMEM
SMEM = pltpu.SMEM


def plane_of(ref, a, d):
    return ref[pl.ds(2 * d + a, Z, stride=4), :]


def dot_full(left, right):
    return jnp.dot(left, right, precision=HIGHEST_PREC, preferred_element_type=jnp.float32)


def split_lanes(wide, count):
    return [wide[:, i * LANES : (i + 1) * LANES] for i in range(count)]


def expect_kernel(value_ref, transition_ref, shock_ref, expected_ref):
    rows = lax.broadcasted_iota(jnp.int32, (Z, Z), 0)
    cols = lax.broadcasted_iota(jnp.int32, (Z, Z), 1)
    scale = jnp.where(rows == cols, shock_ref[...] * (DISCOUNT * GROSS_RATE), 0.0)
    scaled = dot_full(scale, transition_ref[...])
    planes = [plane_of(value_ref, p // 2, p % 2) for p in range(4)]
    expected = dot_full(scaled, jnp.concatenate(planes, axis=1))
    for p, plane in enumerate(split_lanes(expected, 4)):
        expected_ref[p * Z : (p + 1) * Z, :] = plane


def interpolate(pieces, index, weight, me):
    upper_index = index + 1
    quarter = ((index >> 7) - me) & 3
    upper_quarter = ((upper_index >> 7) - me) & 3
    lane = index & 127
    upper_lane = upper_index & 127
    lower = upper = None
    for q, piece in enumerate(pieces):
        low = jnp.take_along_axis(piece, lane, axis=1, mode="promise_in_bounds")
        high = jnp.take_along_axis(piece, upper_lane, axis=1, mode="promise_in_bounds")
        lower = low if lower is None else jnp.where(quarter == q, low, lower)
        upper = high if upper is None else jnp.where(upper_quarter == q, high, upper)
    return weight * lower + (1.0 - weight) * upper


def policy_plane(own, above, drift, index, weight, me):
    endogenous = [lax.rsqrt(drift * o + (1.0 - drift) * u) for o, u in zip(own, above)]
    return interpolate(endogenous, index, weight, me)


def forward_half(
    a, own, above, drift, me, transition_ref,
    index_ref, weight_ref, steady_ref, lottery_ref, target_ref, population_ref,
    mass_scr, row_scr,
):
    values = []
    for d in range(2):
        index = plane_of(index_ref, a, d)
        weight = plane_of(weight_ref, a, d)
        policy = policy_plane(own[d], above[d], drift, index, weight, me)
        values.append(GROSS_RATE / (policy * policy))
        share = plane_of(lottery_ref, a, d) + SLOPE_GAIN * (policy - plane_of(steady_ref, a, d))
        share = jnp.clip(share, 0.0, 1.0)
        population = plane_of(population_ref, a, d)
        rows = slice(d * Z, (d + 1) * Z)
        mass_scr[0, rows, :] = population * share
        mass_scr[1, rows, :] = population * (1.0 - share)
    scaled = transition_ref[...] * (DISCOUNT * GROSS_RATE)
    expected = split_lanes(dot_full(scaled, jnp.concatenate(values, axis=1)), 2)

    sub8 = lax.broadcasted_iota(jnp.int32, (8, LANES), 0)
    is_low = sub8 < 4
    sub_quarter = sub8 & 3
    sub128 = lax.broadcasted_iota(jnp.int32, (LANES, LANES), 0)
    for d in range(2):
        for z in range(Z):
            row = d * Z + z
            target = target_ref[pl.ds(4 * z + 2 * d + a, 1), :]
            quarter = ((target >> 7) - me) & 3
            hot = jnp.where(sub128 == (target & 127), 1.0, 0.0).astype(jnp.bfloat16)
            mass = jnp.where(is_low, mass_scr[0, row : row + 1, :], mass_scr[1, row : row + 1, :])
            mass = jnp.where(quarter == sub_quarter, mass, 0.0)
            first = mass.astype(jnp.bfloat16)
            rest = mass - first.astype(jnp.float32)
            both = jnp.concatenate([mass, rest], axis=0).astype(jnp.bfloat16)
            out = lax.dot_general(both, hot, (((1,), (1,)), ((), ())), preferred_element_type=jnp.float32)
            row_scr[row * 8 : row * 8 + 8, :] = out[:8] + out[8:]
    lane = lax.broadcasted_iota(jnp.int32, (HALF_ROWS, LANES), 1)
    low = [row_scr[pl.ds(q, HALF_ROWS, stride=8), :] for q in range(4)]
    high = [pltpu.roll(row_scr[pl.ds(4 + q, HALF_ROWS, stride=8), :], 1, 1) for q in range(4)]
    rows_by_quarter = [low[q] + jnp.where(lane == 0, high[(q + 3) % 4], high[q]) for q in range(4)]
    return expected, rows_by_quarter


def rows_of(refs, p):
    return [ref[p * Z : (p + 1) * Z, :] for ref in refs]


def first_half_kernel(
    ints_ref, floats_ref, e0, e1, e2, e3, transition_ref, index_ref, weight_ref, steady_ref, lottery_ref, target_ref,
    population_ref, out_ref, mass_scr, row_scr,
):
    pieces = (e0, e1, e2, e3)
    expected, by_quarter = forward_half(
        0, [rows_of(pieces, 0), rows_of(pieces, 1)], [rows_of(pieces, 2), rows_of(pieces, 3)], floats_ref[0],
        ints_ref[0], transition_ref, index_ref, weight_ref, steady_ref, lottery_ref, target_ref, population_ref,
        mass_scr, row_scr,
    )
    for q in range(4):
        out_ref[q * HALF_ROWS : (q + 1) * HALF_ROWS, :] = by_quarter[q]
    for d in range(2):
        out_ref[4 * HALF_ROWS + d * Z : 4 * HALF_ROWS + (d + 1) * Z, :] = expected[d]


def second_half_kernel(
    ints_ref, floats_ref, e0, e1, e2, e3, halo_ref, first_ref, transition_ref, index_ref, weight_ref, steady_ref,
    lottery_ref, target_ref, population_ref, p0, p1, p2, p3, mass_scr, row_scr,
):
    pieces = (e0, e1, e2, e3)
    above = [[halo_ref[q * HALF_ROWS + d * Z : q * HALF_ROWS + (d + 1) * Z, :] for q in range(4)] for d in range(2)]
    expected, by_quarter = forward_half(
        1, [rows_of(pieces, 2), rows_of(pieces, 3)], above, floats_ref[1],
        ints_ref[0], transition_ref, index_ref, weight_ref, steady_ref, lottery_ref, target_ref, population_ref,
        mass_scr, row_scr,
    )
    for q, out in enumerate((p0, p1, p2, p3)):
        out[:HALF_ROWS, :] = first_ref[q * HALF_ROWS : (q + 1) * HALF_ROWS, :]
        out[HALF_ROWS : 2 * HALF_ROWS, :] = by_quarter[q]
        out[2 * HALF_ROWS : 3 * HALF_ROWS, :] = first_ref[4 * HALF_ROWS :, :]
        for d in range(2):
            out[3 * HALF_ROWS + d * Z : 3 * HALF_ROWS + (d + 1) * Z, :] = expected[d]


def consume_kernel(ints_ref, floats_ref, e0, e1, e2, e3, halo_ref, index_ref, weight_ref, out_ref):
    pieces = (e0, e1, e2, e3)
    for a in range(2):
        for d in range(2):
            own = [ref[PLANE_ROWS + (2 * a + d) * Z : PLANE_ROWS + (2 * a + d + 1) * Z, :] for ref in pieces]
            if a == 0:
                above = [ref[PLANE_ROWS + (2 + d) * Z : PLANE_ROWS + (3 + d) * Z, :] for ref in pieces]
            else:
                above = [halo_ref[q * HALF_ROWS + d * Z : q * HALF_ROWS + (d + 1) * Z, :] for q in range(4)]
            policy = policy_plane(
                own, above, floats_ref[a], plane_of(index_ref, a, d), plane_of(weight_ref, a, d), ints_ref[0]
            )
            out_ref[pl.ds(2 * d + a, Z, stride=4), :] = policy


def gather_mass_kernel(floats_ref, p0, p1, p2, p3, ill_ref, core_out, dur_out):
    total = p0[:PLANE_ROWS, :] + p1[:PLANE_ROWS, :] + p2[:PLANE_ROWS, :] + p3[:PLANE_ROWS, :]
    target = jnp.broadcast_to(ill_ref[...].astype(jnp.float32), (8, LANES))
    core_out[:PLANE_ROWS, :] = total
    core_out[PLANE_ROWS:, :] = target
    leave = floats_ref[4]
    dur_out[:Z, :] = leave * total[:Z]
    dur_out[Z : 2 * Z, :] = leave * total[2 * Z : 3 * Z]
    dur_out[2 * Z :, :] = target


def spread_targets(target_row, planes):
    z = lax.broadcasted_iota(jnp.int32, (Z, LANES), 0)
    lane = lax.broadcasted_iota(jnp.int32, (Z, LANES), 1)
    picked = [jnp.where(lane == 4 * z + 2 * d + a, target_row, 0.0) for a, d in planes]
    picked = jnp.concatenate(picked, axis=0).astype(jnp.bfloat16)
    ones = jnp.ones((LANES, LANES), jnp.bfloat16)
    return jnp.dot(picked, ones, preferred_element_type=jnp.float32)


def settle_kernel(ints_ref, floats_ref, own_ref, core_ref, dur_ref, dur_core_ref, o0, o1, o2, o3):
    whole = ((0, 0), (0, 1), (1, 0), (1, 1))
    lowest = ((0, 0), (1, 0))
    sources = ([], [])
    for ref in (own_ref, core_ref):
        targets = spread_targets(ref[PLANE_ROWS : PLANE_ROWS + 1, :], whole)
        for p, (_, d) in enumerate(whole):
            sources[d].append((targets[p * Z : (p + 1) * Z], ref[p * Z : (p + 1) * Z, :]))
    arriving = []
    for ref in (dur_ref, dur_core_ref):
        targets = spread_targets(ref[2 * Z : 2 * Z + 1, :], lowest)
        for p in range(2):
            arriving.append((targets[p * Z : (p + 1) * Z], ref[p * Z : (p + 1) * Z, :]))
    y, core = ints_ref[1], ints_ref[2]
    stay_low, stay_high, leave_high = floats_ref[2], floats_ref[3], floats_ref[5]
    for k, out in enumerate((o0, o1, o2, o3)):
        for a in range(2):
            point = (4 * ((y + k) & 3) + 2 * core + a).astype(jnp.float32)

            def gathered(pairs):
                parts = [jnp.where(target == point, mass, 0.0) for target, mass in pairs]
                return (parts[0] + parts[1]) + (parts[2] + parts[3])

            low, high = gathered(sources[0]), gathered(sources[1])
            out[2 * a * Z : (2 * a + 1) * Z, :] = stay_low * low + leave_high * high
            out[(2 * a + 1) * Z : (2 * a + 2) * Z, :] = stay_high * high + gathered(arriving)


def population_kernel(transition_ref, s0, s1, s2, s3, out_ref):
    settled = (s0[...] + s1[...]) + (s2[...] + s3[...])
    wide = jnp.concatenate([settled[p * Z : (p + 1) * Z] for p in range(4)], axis=1)
    moved = lax.dot_general(
        transition_ref[...], wide, (((0,), (0,)), ((), ())), precision=HIGHEST_PREC, preferred_element_type=jnp.float32
    )
    for p, plane in enumerate(split_lanes(moved, 4)):
        a, d = p // 2, p % 2
        out_ref[pl.ds(2 * d + a, Z, stride=4), :] = plane


def call(kernel, out_rows, spaces, scratch=()):
    shapes = [jax.ShapeDtypeStruct((rows, LANES), jnp.float32) for rows in out_rows]
    specs = [pl.BlockSpec(memory_space=VMEM) for _ in out_rows]
    single = len(out_rows) == 1
    return pl.pallas_call(
        kernel,
        out_shape=shapes[0] if single else shapes,
        in_specs=[pl.BlockSpec(memory_space=SMEM if s == "s" else VMEM) for s in spaces],
        out_specs=specs[0] if single else specs,
        scratch_shapes=list(scratch),
    )


def turned(axis, distance):
    count = lax.axis_size(axis)
    return [(i, (i + distance) % count) for i in range(count)]


def from_other_liq(pieces):
    got = [lax.ppermute(pieces[k], "liq", turned("liq", k)) for k in range(1, 4)]
    return [got[3 - k] for k in range(1, 4)]


def from_above_ill(x):
    return lax.ppermute(x, "ill", turned("ill", -1))


def body(
    marginal_value, transition, discount_shock, illiquid_drift, durable_keep, bracket_index, bracket_weight,
    steady_consumption, lottery_weight, liquid_target, illiquid_target, population,
):
    flat = lambda x: x.reshape(PLANE_ROWS, LANES)
    liq, ill, dur = lax.axis_index("liq"), lax.axis_index("ill"), lax.axis_index("dur")
    ill_count, dur_count = lax.axis_size("ill"), lax.axis_size("dur")
    ints = jnp.stack([liq, ill // 2, ill % 2]).astype(jnp.int32)
    last = ill == ill_count - 1
    stay_low = jnp.where(dur == 0, 1.0, durable_keep[0])
    stay_high = durable_keep[1]
    floats = jnp.stack(
        [
            illiquid_drift[0],
            jnp.where(last, 1.0, illiquid_drift[1]),
            stay_low,
            stay_high,
            1.0 - stay_low,
            1.0 - stay_high,
        ]
    )
    index, weight = flat(bracket_index), flat(bracket_weight)
    states = [index, weight] + [flat(x) for x in (steady_consumption, lottery_weight, liquid_target, population)]
    scratch = [pltpu.VMEM((2, HALF_ROWS, LANES), jnp.float32), pltpu.VMEM((8 * HALF_ROWS, LANES), jnp.float32)]

    with jax.named_scope("expect"):
        expected = call(expect_kernel, [PLANE_ROWS], "vvv")(
            flat(marginal_value), transition, discount_shock.reshape(1, Z)
        )
    with jax.named_scope("expected_over_liq"):
        pieces = [expected] + from_other_liq([expected] * 4)
    with jax.named_scope("expected_over_ill"):
        halo = from_above_ill(jnp.concatenate([x[:HALF_ROWS] for x in pieces], axis=0))
    with jax.named_scope("first_half"):
        first = call(first_half_kernel, [5 * HALF_ROWS], "ss" + "v" * 11, scratch)(
            ints, floats, *pieces, transition, *states
        )
    with jax.named_scope("second_half"):
        sends = call(second_half_kernel, [4 * HALF_ROWS] * 4, "ss" + "v" * 13, scratch)(
            ints, floats, *pieces, halo, first, transition, *states
        )
    with jax.named_scope("mass_over_liq"):
        got = [sends[0]] + from_other_liq(sends)
    with jax.named_scope("gather_mass"):
        to_core, to_dur = call(gather_mass_kernel, [PLANE_ROWS + 8, HALF_ROWS + 8], "s" + "v" * 5)(
            floats, *got, illiquid_target.reshape(1, PLANE_ROWS)
        )
    with jax.named_scope("mass_over_core_and_dur"):
        other_core = [(i, i ^ 1) for i in range(ill_count)]
        both = [
            (i * dur_count + d, (i ^ 1) * dur_count + (d - 1) % dur_count)
            for i in range(ill_count)
            for d in range(dur_count)
        ]
        from_core = lax.ppermute(to_core, "ill", other_core)
        from_dur = lax.ppermute(to_dur, "dur", turned("dur", -1))
        from_dur_core = lax.ppermute(to_dur, ("ill", "dur"), both)
    with jax.named_scope("expected_over_ill"):
        halo = from_above_ill(
            jnp.concatenate([x[PLANE_ROWS : PLANE_ROWS + HALF_ROWS] for x in got], axis=0)
        )
    with jax.named_scope("settle"):
        parts = call(settle_kernel, [PLANE_ROWS] * 4, "ssvvvv")(
            ints, floats, to_core, from_core, from_dur, from_dur_core
        )
    with jax.named_scope("mass_over_ill"):
        arrived = [lax.ppermute(parts[k], "ill", turned("ill", 2 * k)) for k in range(1, 4)]
    with jax.named_scope("consume"):
        consumption = call(consume_kernel, [PLANE_ROWS], "ss" + "v" * 7)(ints, floats, *got, halo, index, weight)
    with jax.named_scope("population"):
        population_next = call(population_kernel, [PLANE_ROWS], "vvvvv")(transition, parts[0], *arrived)
    shape = population.shape
    return consumption.reshape(shape), population_next.reshape(shape)


def solution(mesh):
    state = P(None, "dur", "ill", "liq")
    in_specs = (
        state, P(), P(), P("ill"), P("dur"), state, state, state, state, state, P(None, "dur", "ill"), state,
    )
    return jax.shard_map(body, mesh=mesh, in_specs=in_specs, out_specs=(state, state), check_vma=False)
```

```python
import functools

import jax
import jax.numpy as jnp
from jax import lax
from jax.experimental import pallas as pl
from jax.experimental.pallas import tpu as pltpu
from jax.sharding import PartitionSpec as P

DISCOUNT = 0.96
GROSS_RATE = 1.01
SLOPE_GAIN = 0.5
HIGHEST_PREC = lax.Precision.HIGHEST

Z = 32
LANES = 128
PLANE_ROWS = 4 * Z
HALF_ROWS = 2 * Z
KERNEL_VMEM = 4 << 20
VMEM = pltpu.VMEM
SMEM = pltpu.SMEM


def plane_of(ref, a, d):
    return ref[pl.ds(2 * d + a, Z, stride=4), :]


def dot_full(left, right):
    return jnp.dot(left, right, precision=HIGHEST_PREC, preferred_element_type=jnp.float32)


def split_lanes(wide, count):
    return [wide[:, i * LANES : (i + 1) * LANES] for i in range(count)]


def pack_kernel(v0, v1, v2, v3, out_ref):
    for q, ref in enumerate((v1, v2, v3)):
        for d in range(2):
            out_ref[(q + 1) * HALF_ROWS + d * Z : (q + 1) * HALF_ROWS + (d + 1) * Z, :] = plane_of(ref, 0, d)
    out_ref[:HALF_ROWS, :] = v0[:HALF_ROWS, :]


def interpolate(pieces, index, weight, me):
    upper_index = index + 1
    quarter = ((index >> 7) - me) & 3
    upper_quarter = ((upper_index >> 7) - me) & 3
    lane = index & 127
    upper_lane = upper_index & 127
    lower = upper = None
    for q, piece in enumerate(pieces):
        low = jnp.take_along_axis(piece, lane, axis=1, mode="promise_in_bounds")
        high = jnp.take_along_axis(piece, upper_lane, axis=1, mode="promise_in_bounds")
        lower = low if lower is None else jnp.where(quarter == q, low, lower)
        upper = high if upper is None else jnp.where(upper_quarter == q, high, upper)
    return weight * lower + (1.0 - weight) * upper


def policy_plane(own, above, drift, index, weight, me):
    endogenous = [lax.rsqrt(drift * o + (1.0 - drift) * u) for o, u in zip(own, above)]
    return interpolate(endogenous, index, weight, me)


def forward_half(
    a, own, above, drift, me, transition_ref,
    index_ref, weight_ref, steady_ref, lottery_ref, target_ref, population_ref,
    mass_scr, row_scr,
):
    values = []
    for d in range(2):
        index = plane_of(index_ref, a, d)
        weight = plane_of(weight_ref, a, d)
        policy = policy_plane(own[d], above[d], drift, index, weight, me)
        values.append(GROSS_RATE / (policy * policy))
        share = plane_of(lottery_ref, a, d) + SLOPE_GAIN * (policy - plane_of(steady_ref, a, d))
        share = jnp.clip(share, 0.0, 1.0)
        population = plane_of(population_ref, a, d)
        rows = slice(d * Z, (d + 1) * Z)
        mass_scr[0, rows, :] = population * share
        mass_scr[1, rows, :] = population * (1.0 - share)
    scaled = transition_ref[...] * (DISCOUNT * GROSS_RATE)
    expected = split_lanes(dot_full(scaled, jnp.concatenate(values, axis=1)), 2)

    sub8 = lax.broadcasted_iota(jnp.int32, (8, LANES), 0)
    is_low = sub8 < 4
    sub_quarter = sub8 & 3
    sub128 = lax.broadcasted_iota(jnp.int32, (LANES, LANES), 0)
    for d in range(2):
        for z in range(Z):
            row = d * Z + z
            target = target_ref[pl.ds(4 * z + 2 * d + a, 1), :]
            quarter = ((target >> 7) - me) & 3
            hot = jnp.where(sub128 == (target & 127), 1.0, 0.0).astype(jnp.bfloat16)
            mass = jnp.where(is_low, mass_scr[0, row : row + 1, :], mass_scr[1, row : row + 1, :])
            mass = jnp.where(quarter == sub_quarter, mass, 0.0)
            first = mass.astype(jnp.bfloat16)
            rest = mass - first.astype(jnp.float32)
            both = jnp.concatenate([mass, rest], axis=0).astype(jnp.bfloat16)
            out = lax.dot_general(both, hot, (((1,), (1,)), ((), ())), preferred_element_type=jnp.float32)
            row_scr[row * 8 : row * 8 + 8, :] = out[:8] + out[8:]
    lane = lax.broadcasted_iota(jnp.int32, (HALF_ROWS, LANES), 1)
    low = [row_scr[pl.ds(q, HALF_ROWS, stride=8), :] for q in range(4)]
    high = [pltpu.roll(row_scr[pl.ds(4 + q, HALF_ROWS, stride=8), :], 1, 1) for q in range(4)]
    rows_by_quarter = [low[q] + jnp.where(lane == 0, high[(q + 3) % 4], high[q]) for q in range(4)]
    return expected, rows_by_quarter


def last_drift(drift_ref):
    is_last = lax.axis_index("ill") == lax.axis_size("ill") - 1
    return jnp.where(is_last, 1.0, drift_ref[1])


def stay_of(keep_ref):
    return jnp.where(lax.axis_index("dur") == 0, 1.0, keep_ref[0]), keep_ref[1]


def rows_of(refs, p):
    return [ref[p * Z : (p + 1) * Z, :] for ref in refs]


def rows_of(refs, p):
    return [ref[p * Z : (p + 1) * Z, :] for ref in refs]


def first_half_kernel(
    small_ref, v0, v1, v2, v3, scaled_ref, transition_ref, index_ref, weight_ref, steady_ref, lottery_ref, target_ref,
    population_ref, mass_ref, expected_ref, upper_ref, mass_scr, row_scr,
):
    values = []
    for p in range(4):
        values += [v0[p * Z : (p + 1) * Z, :]] + [plane_of(ref, p // 2, p % 2) for ref in (v1, v2, v3)]
    planes = split_lanes(dot_full(scaled_ref[...], jnp.concatenate(values, axis=1)), 16)
    for i in range(8):
        upper_ref[i * Z : (i + 1) * Z, :] = planes[8 + i]
    expected, by_quarter = forward_half(
        0, [planes[0:4], planes[4:8]], [planes[8:12], planes[12:16]], small_ref[0:1, :],
        lax.axis_index("liq"), transition_ref, index_ref, weight_ref, steady_ref, lottery_ref, target_ref,
        population_ref, mass_scr, row_scr,
    )
    for q in range(4):
        mass_ref[q * HALF_ROWS : (q + 1) * HALF_ROWS, :] = by_quarter[q]
    for d in range(2):
        expected_ref[d * Z : (d + 1) * Z, :] = expected[d]


def second_half_kernel(
    small_ref, upper_ref, halo_ref, first_ref, scaled_ref, transition_ref, index_ref, weight_ref, steady_ref,
    lottery_ref, target_ref, population_ref, p0, p1, p2, p3, expected_ref, mass_scr, row_scr,
):
    own = [[upper_ref[(4 * d + q) * Z : (4 * d + q + 1) * Z, :] for q in range(4)] for d in range(2)]
    values = [halo_ref[q * HALF_ROWS + d * Z : q * HALF_ROWS + (d + 1) * Z, :] for d in range(2) for q in range(4)]
    planes = split_lanes(dot_full(scaled_ref[...], jnp.concatenate(values, axis=1)), 8)
    expected, by_quarter = forward_half(
        1, own, [planes[0:4], planes[4:8]], small_ref[1:2, :],
        lax.axis_index("liq"), transition_ref, index_ref, weight_ref, steady_ref, lottery_ref, target_ref,
        population_ref, mass_scr, row_scr,
    )
    for q, out in enumerate((p0, p1, p2, p3)):
        out[:HALF_ROWS, :] = first_ref[q * HALF_ROWS : (q + 1) * HALF_ROWS, :]
        out[HALF_ROWS:, :] = by_quarter[q]
    for d in range(2):
        expected_ref[d * Z : (d + 1) * Z, :] = expected[d]


def consume_kernel(small_ref, e0, e1, e2, e3, index_ref, weight_ref, out_ref):
    pieces = (e0, e1, e2, e3)
    for a in range(2):
        for d in range(2):
            policy = policy_plane(
                rows_of(pieces, 2 * a + d), rows_of(pieces, 2 * a + 2 + d), small_ref[a : a + 1, :],
                plane_of(index_ref, a, d), plane_of(weight_ref, a, d), lax.axis_index("liq"),
            )
            out_ref[pl.ds(2 * d + a, Z, stride=4), :] = policy


def gather_mass_kernel(small_ref, p0, p1, p2, p3, lower_ref, upper_ref, halo_ref, core_out, expected_out):
    core_out[:PLANE_ROWS, :] = (p0[...] + p1[...]) + (p2[...] + p3[...])
    core_out[PLANE_ROWS:, :] = small_ref[...]
    for i, ref in enumerate((lower_ref, upper_ref, halo_ref)):
        expected_out[i * HALF_ROWS : (i + 1) * HALF_ROWS, :] = ref[...]


def leave_kernel(own_ref, core_ref, dur_out):
    for i, ref in enumerate((own_ref, core_ref)):
        leave = 1.0 - ref[PLANE_ROWS + 2 : PLANE_ROWS + 3, :]
        for a in range(2):
            row = i * HALF_ROWS + a * Z
            dur_out[row : row + Z, :] = leave * ref[2 * a * Z : (2 * a + 1) * Z, :]
        dur_out[PLANE_ROWS + 8 * i : PLANE_ROWS + 8 * i + 8, :] = ref[PLANE_ROWS:, :]


def spread_targets(small):
    rows = lax.broadcasted_iota(jnp.int32, (Z, LANES), 0)
    lane = lax.broadcasted_iota(jnp.int32, (Z, LANES), 1)
    picked = [jnp.where(lane == rows, row, 0.0) for row in small]
    picked = jnp.concatenate(picked, axis=0).astype(jnp.bfloat16)
    ones = jnp.ones((LANES, LANES), jnp.bfloat16)
    return jnp.dot(picked, ones, preferred_element_type=jnp.float32)


def settle_kernel(own_ref, core_ref, dur_ref, o0, o1, o2, o3):
    sources = ([], [])
    for ref in (own_ref, core_ref):
        targets = spread_targets([ref[PLANE_ROWS + 4 + p : PLANE_ROWS + 5 + p, :] for p in range(4)])
        for p in range(4):
            sources[p % 2].append((targets[p * Z : (p + 1) * Z], ref[p * Z : (p + 1) * Z, :]))
    arriving = []
    targets = spread_targets(
        [dur_ref[PLANE_ROWS + i + p : PLANE_ROWS + i + p + 1, :] for i in (4, 12) for p in (0, 2)]
    )
    for i in range(4):
        arriving.append((targets[i * Z : (i + 1) * Z], dur_ref[i * Z : (i + 1) * Z, :]))
    ill = lax.axis_index("ill")
    y, core = ill >> 1, ill & 1
    stay_low, stay_high = own_ref[PLANE_ROWS + 2 : PLANE_ROWS + 3, :], own_ref[PLANE_ROWS + 3 : PLANE_ROWS + 4, :]
    leave_high = 1.0 - stay_high
    for k, out in enumerate((o0, o1, o2, o3)):
        for a in range(2):
            point = (4 * ((y + k) & 3) + 2 * core + a).astype(jnp.float32)

            def gathered(pairs):
                parts = [jnp.where(target == point, mass, 0.0) for target, mass in pairs]
                return (parts[0] + parts[1]) + (parts[2] + parts[3])

            low, high = gathered(sources[0]), gathered(sources[1])
            out[2 * a * Z : (2 * a + 1) * Z, :] = stay_low * low + leave_high * high
            out[(2 * a + 1) * Z : (2 * a + 2) * Z, :] = stay_high * high + gathered(arriving)


def population_kernel(transition_ref, s0, s1, s2, s3, out_ref):
    settled = (s0[...] + s1[...]) + (s2[...] + s3[...])
    wide = jnp.concatenate([settled[p * Z : (p + 1) * Z] for p in range(4)], axis=1)
    moved = lax.dot_general(
        transition_ref[...], wide, (((0,), (0,)), ((), ())), precision=HIGHEST_PREC, preferred_element_type=jnp.float32
    )
    for p, plane in enumerate(split_lanes(moved, 4)):
        a, d = p // 2, p % 2
        out_ref[pl.ds(2 * d + a, Z, stride=4), :] = plane


def call(kernel, out_rows, inputs, scratch=(), work=0):
    shapes = [jax.ShapeDtypeStruct(rows if isinstance(rows, tuple) else (rows, LANES), jnp.float32) for rows in out_rows]
    specs = [pl.BlockSpec(memory_space=VMEM) for _ in out_rows]
    single = len(out_rows) == 1
    return pl.pallas_call(
        kernel,
        out_shape=shapes[0] if single else shapes,
        in_specs=[pl.BlockSpec(memory_space=VMEM)] * len(inputs),
        out_specs=specs[0] if single else specs,
        scratch_shapes=list(scratch),
        compiler_params=pltpu.CompilerParams(vmem_limit_bytes=KERNEL_VMEM),
        cost_estimate=pl.CostEstimate(flops=0, transcendentals=0, bytes_accessed=work) if work else None,
    )(*inputs)


def turned(axis, distance):
    count = lax.axis_size(axis)
    return [(i, (i + distance) % count) for i in range(count)]


def from_other_liq(pieces):
    got = [lax.ppermute(pieces[k], "liq", turned("liq", k)) for k in range(1, 4)]
    return [got[3 - k] for k in range(1, 4)]


def from_above_ill(x):
    return lax.ppermute(x, "ill", turned("ill", -1))


def body(
    marginal_value, transition, discount_shock, illiquid_drift, durable_keep, bracket_index, bracket_weight,
    steady_consumption, lottery_weight, liquid_target, illiquid_target, population,
):
    flat = lambda x: x.reshape(PLANE_ROWS, LANES)
    ill_count, dur_count = lax.axis_size("ill"), lax.axis_size("dur")
    index, weight = flat(bracket_index), flat(bracket_weight)
    states = [index, weight] + [flat(x) for x in (steady_consumption, lottery_weight, liquid_target, population)]
    scratch = [pltpu.VMEM((2, HALF_ROWS, LANES), jnp.float32), pltpu.VMEM((8 * HALF_ROWS, LANES), jnp.float32)]
    below_dur = [(d, d - 1) for d in range(1, dur_count)]
    other_core = [(i, i ^ 1) for i in range(ill_count)]

    with jax.named_scope("value_over_liq"):
        value = flat(marginal_value)
        pieces = [marginal_value.transpose(2, 1, 0, 3).reshape(PLANE_ROWS, LANES)] + from_other_liq([value] * 4)
    with jax.named_scope("prepare"):
        scaled = transition * (discount_shock * (DISCOUNT * GROSS_RATE))[:, None]
        is_last = lax.axis_index("ill") == ill_count - 1
        is_lowest = lax.axis_index("dur") == 0
        row = lax.broadcasted_iota(jnp.int32, (8, LANES), 0)
        drift = jnp.where(row[:2] == 0, illiquid_drift[:, None], jnp.where(is_last, 1.0, illiquid_drift[:, None]))
        stay = jnp.where((row[:2] == 0) & is_lowest, 1.0, durable_keep[:, None])
        target = illiquid_target.transpose(2, 1, 0).reshape(4, Z).astype(jnp.float32)
        small = jnp.concatenate([drift, stay, jnp.pad(target, ((0, 0), (0, LANES - Z)))], axis=0)
    with jax.named_scope("value_over_ill"):
        halo = from_above_ill(call(pack_kernel, [4 * HALF_ROWS], pieces))
    with jax.named_scope("first_half"):
        mass, lower, upper = call(
            first_half_kernel,
            [4 * HALF_ROWS, HALF_ROWS, 4 * HALF_ROWS],
            [small, *pieces, scaled, transition, *states],
            scratch,
        )
    with jax.named_scope("expected_over_ill"):
        next_halo = from_above_ill(lower)
    with jax.named_scope("second_half"):
        *sends, higher = call(
            second_half_kernel,
            [PLANE_ROWS] * 4 + [HALF_ROWS],
            [small, upper, halo, mass, scaled, transition, *states],
            scratch,
            30000000,
        )
    with jax.named_scope("mass_over_liq"):
        got = [sends[0]] + from_other_liq(sends)
    with jax.named_scope("gather_mass"):
        to_core, expected = call(
            gather_mass_kernel, [PLANE_ROWS + 8, 3 * HALF_ROWS], [small, *got, lower, higher, next_halo]
        )
    with jax.named_scope("mass_over_core"):
        from_core = lax.ppermute(to_core, "ill", other_core)
    with jax.named_scope("leave"):
        to_dur = call(leave_kernel, [PLANE_ROWS + 16], [to_core, from_core])
    with jax.named_scope("mass_over_dur"):
        from_dur = lax.ppermute(to_dur, "dur", below_dur)
    with jax.named_scope("expected_over_liq"):
        expected_pieces = [expected] + from_other_liq([expected] * 4)
    with jax.named_scope("settle"):
        parts = call(settle_kernel, [PLANE_ROWS] * 4, [to_core, from_core, from_dur])
    with jax.named_scope("mass_over_ill"):
        arrived = [lax.ppermute(parts[k], "ill", turned("ill", 2 * k)) for k in range(1, 4)]
    with jax.named_scope("consume"):
        consumption = call(consume_kernel, [PLANE_ROWS], [small, *expected_pieces, index, weight])
    with jax.named_scope("population"):
        population_next = call(population_kernel, [PLANE_ROWS], [transition, parts[0], *arrived])
    shape = population.shape
    return consumption.reshape(shape), population_next.reshape(shape)


def solution(mesh):
    state = P(None, "dur", "ill", "liq")
    in_specs = (
        state, P(), P(), P("ill"), P("dur"), state, state, state, state, state, P(None, "dur", "ill"), state,
    )
    return jax.shard_map(body, mesh=mesh, in_specs=in_specs, out_specs=(state, state), check_vma=False)
```

```python
import functools

import jax
import jax.numpy as jnp
from jax import lax
from jax.experimental import pallas as pl
from jax.experimental.pallas import tpu as pltpu
from jax.sharding import PartitionSpec as P

DISCOUNT = 0.96
GROSS_RATE = 1.01
SLOPE_GAIN = 0.5
HIGHEST_PREC = lax.Precision.HIGHEST

Z = 32
LANES = 128
PLANE_ROWS = 4 * Z
HALF_ROWS = 2 * Z
KERNEL_VMEM = 4 << 20
VMEM = pltpu.VMEM
SMEM = pltpu.SMEM


def plane_of(ref, a, d):
    return ref[pl.ds(2 * d + a, Z, stride=4), :]


def dot_full(left, right):
    return jnp.dot(left, right, precision=HIGHEST_PREC, preferred_element_type=jnp.float32)


def split_lanes(wide, count):
    return [wide[:, i * LANES : (i + 1) * LANES] for i in range(count)]


def pack_kernel(v0, v1, v2, v3, hot_ref, out_ref):
    del hot_ref
    for q, ref in enumerate((v1, v2, v3)):
        for d in range(2):
            out_ref[(q + 1) * HALF_ROWS + d * Z : (q + 1) * HALF_ROWS + (d + 1) * Z, :] = plane_of(ref, 0, d)
    out_ref[:HALF_ROWS, :] = v0[:HALF_ROWS, :]


def interpolate(pieces, index, weight, me):
    upper_index = index + 1
    quarter = ((index >> 7) - me) & 3
    upper_quarter = ((upper_index >> 7) - me) & 3
    lane = index & 127
    upper_lane = upper_index & 127
    lower = upper = None
    for q, piece in enumerate(pieces):
        low = jnp.take_along_axis(piece, lane, axis=1, mode="promise_in_bounds")
        high = jnp.take_along_axis(piece, upper_lane, axis=1, mode="promise_in_bounds")
        lower = low if lower is None else jnp.where(quarter == q, low, lower)
        upper = high if upper is None else jnp.where(upper_quarter == q, high, upper)
    return weight * lower + (1.0 - weight) * upper


def policy_plane(own, above, drift, index, weight, me):
    endogenous = [lax.rsqrt(drift * o + (1.0 - drift) * u) for o, u in zip(own, above)]
    return interpolate(endogenous, index, weight, me)


def forward_half(
    a, own, above, drift, me, table_ref,
    index_ref, weight_ref, steady_ref, lottery_ref, target_ref, population_ref,
    mass_scr, row_scr, hot_ref=None,
):
    values = []
    for d in range(2):
        index = plane_of(index_ref, a, d)
        weight = plane_of(weight_ref, a, d)
        policy = policy_plane(own[d], above[d], drift, index, weight, me)
        values.append(GROSS_RATE / (policy * policy))
        share = plane_of(lottery_ref, a, d) + SLOPE_GAIN * (policy - plane_of(steady_ref, a, d))
        share = jnp.clip(share, 0.0, 1.0)
        population = plane_of(population_ref, a, d)
        rows = slice(d * Z, (d + 1) * Z)
        mass_scr[0, rows, :] = population * share
        mass_scr[1, rows, :] = population * (1.0 - share)
    scaled = table_ref[8:, :Z] * (DISCOUNT * GROSS_RATE)
    expected = split_lanes(dot_full(scaled, jnp.concatenate(values, axis=1)), 2)

    sub8 = lax.broadcasted_iota(jnp.int32, (8, LANES), 0)
    is_low = sub8 < 4
    sub_quarter = sub8 & 3
    sub128 = lax.broadcasted_iota(jnp.int32, (LANES, LANES), 0)
    for d in range(2):
        for z in range(Z):
            row = d * Z + z
            target = target_ref[pl.ds(4 * z + 2 * d + a, 1), :]
            quarter = ((target >> 7) - me) & 3
            if hot_ref is None:
                hot, hot_lanes = jnp.where(sub128 == (target & 127), 1.0, 0.0).astype(jnp.bfloat16), 1
            else:
                hot, hot_lanes = hot_ref[row * LANES : (row + 1) * LANES, :], 0
            mass = jnp.where(is_low, mass_scr[0, row : row + 1, :], mass_scr[1, row : row + 1, :])
            mass = jnp.where(quarter == sub_quarter, mass, 0.0)
            first = mass.astype(jnp.bfloat16)
            rest = mass - first.astype(jnp.float32)
            both = jnp.concatenate([mass, rest], axis=0).astype(jnp.bfloat16)
            out = lax.dot_general(both, hot, (((1,), (hot_lanes,)), ((), ())), preferred_element_type=jnp.float32)
            row_scr[row * 8 : row * 8 + 8, :] = out[:8] + out[8:]
    lane = lax.broadcasted_iota(jnp.int32, (HALF_ROWS, LANES), 1)
    low = [row_scr[pl.ds(q, HALF_ROWS, stride=8), :] for q in range(4)]
    high = [pltpu.roll(row_scr[pl.ds(4 + q, HALF_ROWS, stride=8), :], 1, 1) for q in range(4)]
    rows_by_quarter = [low[q] + jnp.where(lane == 0, high[(q + 3) % 4], high[q]) for q in range(4)]
    return expected, rows_by_quarter


def last_drift(drift_ref):
    is_last = lax.axis_index("ill") == lax.axis_size("ill") - 1
    return jnp.where(is_last, 1.0, drift_ref[1])


def stay_of(keep_ref):
    return jnp.where(lax.axis_index("dur") == 0, 1.0, keep_ref[0]), keep_ref[1]


def rows_of(refs, p):
    return [ref[p * Z : (p + 1) * Z, :] for ref in refs]


def rows_of(refs, p):
    return [ref[p * Z : (p + 1) * Z, :] for ref in refs]


def hot_kernel(target_ref, out_ref):
    lanes = lax.broadcasted_iota(jnp.int32, (LANES, LANES), 1)
    planes = [plane_of(target_ref, 1, d) & 127 for d in range(2)]
    turned_target = jnp.concatenate(planes + [jnp.zeros((HALF_ROWS, LANES), jnp.int32)], axis=0).T
    for row in range(HALF_ROWS):
        hot = jnp.where(lanes == turned_target[:, row : row + 1], 1.0, 0.0)
        out_ref[row * LANES : (row + 1) * LANES, :] = hot.astype(jnp.bfloat16)


def first_half_kernel(
    table_ref, v0, v1, v2, v3, index_ref, weight_ref, steady_ref, lottery_ref, target_ref,
    population_ref, mass_ref, expected_ref, upper_ref, mass_scr, row_scr,
):
    values = []
    for p in range(4):
        values += [v0[p * Z : (p + 1) * Z, :]] + [plane_of(ref, p // 2, p % 2) for ref in (v1, v2, v3)]
    planes = split_lanes(dot_full(table_ref[8:, :Z] * (table_ref[8:, Z : Z + 1] * (DISCOUNT * GROSS_RATE)), jnp.concatenate(values, axis=1)), 16)
    for i in range(8):
        upper_ref[i * Z : (i + 1) * Z, :] = planes[8 + i]
    expected, by_quarter = forward_half(
        0, [planes[0:4], planes[4:8]], [planes[8:12], planes[12:16]], table_ref[0:1, :],
        lax.axis_index("liq"), table_ref, index_ref, weight_ref, steady_ref, lottery_ref, target_ref,
        population_ref, mass_scr, row_scr,
    )
    for q in range(4):
        mass_ref[q * HALF_ROWS : (q + 1) * HALF_ROWS, :] = by_quarter[q]
    for d in range(2):
        expected_ref[d * Z : (d + 1) * Z, :] = expected[d]


def second_half_kernel(
    table_ref, upper_ref, halo_ref, first_ref, hot_ref, index_ref, weight_ref, steady_ref,
    lottery_ref, target_ref, population_ref, p0, p1, p2, p3, expected_ref, mass_scr, row_scr,
):
    own = [[upper_ref[(4 * d + q) * Z : (4 * d + q + 1) * Z, :] for q in range(4)] for d in range(2)]
    values = [halo_ref[q * HALF_ROWS + d * Z : q * HALF_ROWS + (d + 1) * Z, :] for d in range(2) for q in range(4)]
    planes = split_lanes(dot_full(table_ref[8:, :Z] * (table_ref[8:, Z : Z + 1] * (DISCOUNT * GROSS_RATE)), jnp.concatenate(values, axis=1)), 8)
    expected, by_quarter = forward_half(
        1, own, [planes[0:4], planes[4:8]], table_ref[1:2, :],
        lax.axis_index("liq"), table_ref, index_ref, weight_ref, steady_ref, lottery_ref, target_ref,
        population_ref, mass_scr, row_scr, hot_ref,
    )
    for q, out in enumerate((p0, p1, p2, p3)):
        out[:HALF_ROWS, :] = first_ref[q * HALF_ROWS : (q + 1) * HALF_ROWS, :]
        out[HALF_ROWS:, :] = by_quarter[q]
    for d in range(2):
        expected_ref[d * Z : (d + 1) * Z, :] = expected[d]


def consume_kernel(table_ref, e0, e1, e2, e3, index_ref, weight_ref, out_ref):
    pieces = (e0, e1, e2, e3)
    for a in range(2):
        for d in range(2):
            policy = policy_plane(
                rows_of(pieces, 2 * a + d), rows_of(pieces, 2 * a + 2 + d), table_ref[a : a + 1, :],
                plane_of(index_ref, a, d), plane_of(weight_ref, a, d), lax.axis_index("liq"),
            )
            out_ref[pl.ds(2 * d + a, Z, stride=4), :] = policy


def gather_mass_kernel(table_ref, p0, p1, p2, p3, lower_ref, upper_ref, halo_ref, core_out, expected_out):
    core_out[:PLANE_ROWS, :] = (p0[...] + p1[...]) + (p2[...] + p3[...])
    core_out[PLANE_ROWS:, :] = table_ref[:8, :]
    for i, ref in enumerate((lower_ref, upper_ref, halo_ref)):
        expected_out[i * HALF_ROWS : (i + 1) * HALF_ROWS, :] = ref[...]


def leave_kernel(own_ref, core_ref, dur_out):
    for i, ref in enumerate((own_ref, core_ref)):
        leave = 1.0 - ref[PLANE_ROWS + 2 : PLANE_ROWS + 3, :]
        for a in range(2):
            row = i * HALF_ROWS + a * Z
            dur_out[row : row + Z, :] = leave * ref[2 * a * Z : (2 * a + 1) * Z, :]
        dur_out[PLANE_ROWS + 8 * i : PLANE_ROWS + 8 * i + 8, :] = ref[PLANE_ROWS:, :]


def spread_targets(small):
    rows = lax.broadcasted_iota(jnp.int32, (Z, LANES), 0)
    lane = lax.broadcasted_iota(jnp.int32, (Z, LANES), 1)
    picked = [jnp.where(lane == rows, row, 0.0) for row in small]
    picked = jnp.concatenate(picked, axis=0).astype(jnp.bfloat16)
    ones = jnp.ones((LANES, LANES), jnp.bfloat16)
    return jnp.dot(picked, ones, preferred_element_type=jnp.float32)


def settle_kernel(own_ref, core_ref, dur_ref, o0, o1, o2, o3):
    sources = ([], [])
    for ref in (own_ref, core_ref):
        targets = spread_targets([ref[PLANE_ROWS + row : PLANE_ROWS + row + 1, :] for row in (4, 6, 5, 7)])
        for p in range(4):
            sources[p % 2].append((targets[p * Z : (p + 1) * Z], ref[p * Z : (p + 1) * Z, :]))
    arriving = []
    targets = spread_targets(
        [dur_ref[PLANE_ROWS + row : PLANE_ROWS + row + 1, :] for row in (4, 5, 12, 13)]
    )
    for i in range(4):
        arriving.append((targets[i * Z : (i + 1) * Z], dur_ref[i * Z : (i + 1) * Z, :]))
    ill = lax.axis_index("ill")
    y, core = ill >> 1, ill & 1
    stay_low, stay_high = own_ref[PLANE_ROWS + 2 : PLANE_ROWS + 3, :], own_ref[PLANE_ROWS + 3 : PLANE_ROWS + 4, :]
    leave_high = 1.0 - stay_high
    for k, out in enumerate((o0, o1, o2, o3)):
        for a in range(2):
            point = (4 * ((y + k) & 3) + 2 * core + a).astype(jnp.float32)

            def gathered(pairs):
                parts = [jnp.where(target == point, mass, 0.0) for target, mass in pairs]
                return (parts[0] + parts[1]) + (parts[2] + parts[3])

            low, high = gathered(sources[0]), gathered(sources[1])
            out[2 * a * Z : (2 * a + 1) * Z, :] = stay_low * low + leave_high * high
            out[(2 * a + 1) * Z : (2 * a + 2) * Z, :] = stay_high * high + gathered(arriving)


def population_kernel(table_ref, s0, s1, s2, s3, out_ref):
    settled = (s0[...] + s1[...]) + (s2[...] + s3[...])
    wide = jnp.concatenate([settled[p * Z : (p + 1) * Z] for p in range(4)], axis=1)
    moved = lax.dot_general(
        table_ref[8:, :Z], wide, (((0,), (0,)), ((), ())), precision=HIGHEST_PREC, preferred_element_type=jnp.float32
    )
    for p, plane in enumerate(split_lanes(moved, 4)):
        a, d = p // 2, p % 2
        out_ref[pl.ds(2 * d + a, Z, stride=4), :] = plane


def call(kernel, out_rows, inputs, scratch=(), work=0, dtype=jnp.float32, spaces=None):
    shapes = [jax.ShapeDtypeStruct((rows, LANES), dtype) for rows in out_rows]
    specs = [pl.BlockSpec(memory_space=VMEM) for _ in out_rows]
    single = len(out_rows) == 1
    return pl.pallas_call(
        kernel,
        out_shape=shapes[0] if single else shapes,
        in_specs=[pl.BlockSpec(memory_space=space) for space in spaces or [VMEM] * len(inputs)],
        out_specs=specs[0] if single else specs,
        scratch_shapes=list(scratch),
        compiler_params=pltpu.CompilerParams(vmem_limit_bytes=KERNEL_VMEM),
        cost_estimate=pl.CostEstimate(flops=0, transcendentals=0, bytes_accessed=work) if work else None,
    )(*inputs)


def turned(axis, distance):
    count = lax.axis_size(axis)
    return [(i, (i + distance) % count) for i in range(count)]


def from_other_liq(pieces):
    got = [lax.ppermute(pieces[k], "liq", turned("liq", k)) for k in range(1, 4)]
    return [got[3 - k] for k in range(1, 4)]


def from_above_ill(x):
    return lax.ppermute(x, "ill", turned("ill", -1))


def body(
    marginal_value, transition, discount_shock, illiquid_drift, durable_keep, bracket_index, bracket_weight,
    steady_consumption, lottery_weight, liquid_target, illiquid_target, population,
):
    flat = lambda x: x.reshape(PLANE_ROWS, LANES)
    ill_count, dur_count = lax.axis_size("ill"), lax.axis_size("dur")
    index, weight = flat(bracket_index), flat(bracket_weight)
    states = [index, weight] + [flat(x) for x in (steady_consumption, lottery_weight, liquid_target, population)]
    scratch = [pltpu.VMEM((2, HALF_ROWS, LANES), jnp.float32), pltpu.VMEM((8 * HALF_ROWS, LANES), jnp.float32)]
    below_dur = [(d, d - 1) for d in range(1, dur_count)]
    other_core = [(i, i ^ 1) for i in range(ill_count)]

    with jax.named_scope("value_over_liq"):
        value = flat(marginal_value)
        pieces = [marginal_value.transpose(2, 1, 0, 3).reshape(PLANE_ROWS, LANES)] + from_other_liq([value] * 4)
    with jax.named_scope("prepare"):
        is_last = lax.axis_index("ill") == ill_count - 1
        is_lowest = lax.axis_index("dur") == 0
        row = lax.broadcasted_iota(jnp.int32, (2, LANES), 0)
        drift = jnp.where((row == 1) & is_last, 1.0, illiquid_drift[:, None])
        stay = jnp.where((row == 0) & is_lowest, 1.0, durable_keep[:, None])
        target = illiquid_target.transpose(1, 2, 0).reshape(4, Z).astype(jnp.float32)
        target = jnp.pad(target, ((0, 0), (0, LANES - Z)))
        income = jnp.concatenate(
            [transition, discount_shock[:, None], jnp.zeros((Z, LANES - Z - 1), jnp.float32)], axis=1
        )
        table = jnp.concatenate([drift, stay, target, income], axis=0)
    with jax.named_scope("hot"):
        hot = call(hot_kernel, [HALF_ROWS * LANES], [flat(liquid_target)], dtype=jnp.bfloat16)
    with jax.named_scope("value_over_ill"):
        halo = from_above_ill(call(pack_kernel, [4 * HALF_ROWS], [*pieces, hot], spaces=[VMEM] * 4 + [pl.ANY]))
    with jax.named_scope("first_half"):
        mass, lower, upper = call(
            first_half_kernel,
            [4 * HALF_ROWS, HALF_ROWS, 4 * HALF_ROWS],
            [table, *pieces, *states],
            scratch,
        )
    with jax.named_scope("expected_over_ill"):
        next_halo = from_above_ill(lower)
    with jax.named_scope("second_half"):
        *sends, higher = call(
            second_half_kernel,
            [PLANE_ROWS] * 4 + [HALF_ROWS],
            [table, upper, halo, mass, hot, *states],
            scratch,
            30000000,
        )
    with jax.named_scope("mass_over_liq"):
        got = [sends[0]] + from_other_liq(sends)
    with jax.named_scope("gather_mass"):
        to_core, expected = call(
            gather_mass_kernel, [PLANE_ROWS + 8, 3 * HALF_ROWS], [table, *got, lower, higher, next_halo]
        )
    with jax.named_scope("mass_over_core"):
        from_core = lax.ppermute(to_core, "ill", other_core)
    with jax.named_scope("leave"):
        to_dur = call(leave_kernel, [PLANE_ROWS + 16], [to_core, from_core])
    with jax.named_scope("mass_over_dur"):
        from_dur = lax.ppermute(to_dur, "dur", below_dur)
    with jax.named_scope("expected_over_liq"):
        expected_pieces = [expected] + from_other_liq([expected] * 4)
    with jax.named_scope("settle"):
        parts = call(settle_kernel, [PLANE_ROWS] * 4, [to_core, from_core, from_dur])
    with jax.named_scope("mass_over_ill"):
        arrived = [lax.ppermute(parts[k], "ill", turned("ill", 2 * k)) for k in range(1, 4)]
    with jax.named_scope("consume"):
        consumption = call(consume_kernel, [PLANE_ROWS], [table, *expected_pieces, index, weight])
    with jax.named_scope("population"):
        population_next = call(population_kernel, [PLANE_ROWS], [table, parts[0], *arrived])
    shape = population.shape
    return consumption.reshape(shape), population_next.reshape(shape)


def solution(mesh):
    state = P(None, "dur", "ill", "liq")
    in_specs = (
        state, P(), P(), P("ill"), P("dur"), state, state, state, state, state, P(None, "dur", "ill"), state,
    )
    return jax.shard_map(body, mesh=mesh, in_specs=in_specs, out_specs=(state, state), check_vma=False)
```

```python
import functools

import jax
import jax.numpy as jnp
from jax import lax
from jax.experimental import pallas as pl
from jax.experimental.pallas import tpu as pltpu
from jax.sharding import PartitionSpec as P

DISCOUNT = 0.96
GROSS_RATE = 1.01
SLOPE_GAIN = 0.5
HIGHEST_PREC = lax.Precision.HIGHEST

Z = 32
LANES = 128
PLANE_ROWS = 4 * Z
HALF_ROWS = 2 * Z
KERNEL_VMEM = 4 << 20
VMEM = pltpu.VMEM
SMEM = pltpu.SMEM


def plane_of(ref, a, d):
    return ref[pl.ds(2 * d + a, Z, stride=4), :]


def dot_full(left, right):
    return jnp.dot(left, right, precision=HIGHEST_PREC, preferred_element_type=jnp.float32)


def split_lanes(wide, count):
    return [wide[:, i * LANES : (i + 1) * LANES] for i in range(count)]


def pack_kernel(v0, v1, v2, v3, hot_ref, out_ref):
    del hot_ref
    for q, ref in enumerate((v1, v2, v3)):
        for d in range(2):
            out_ref[(q + 1) * HALF_ROWS + d * Z : (q + 1) * HALF_ROWS + (d + 1) * Z, :] = plane_of(ref, 0, d)
    out_ref[:HALF_ROWS, :] = v0[:HALF_ROWS, :]


def interpolate(pieces, index, weight, me):
    upper_index = index + 1
    quarter = ((index >> 7) - me) & 3
    upper_quarter = ((upper_index >> 7) - me) & 3
    lane = index & 127
    upper_lane = upper_index & 127
    lower = upper = None
    for q, piece in enumerate(pieces):
        low = jnp.take_along_axis(piece, lane, axis=1, mode="promise_in_bounds")
        high = jnp.take_along_axis(piece, upper_lane, axis=1, mode="promise_in_bounds")
        lower = low if lower is None else jnp.where(quarter == q, low, lower)
        upper = high if upper is None else jnp.where(upper_quarter == q, high, upper)
    return weight * lower + (1.0 - weight) * upper


def policy_plane(own, above, drift, index, weight, me):
    endogenous = [lax.rsqrt(drift * o + (1.0 - drift) * u) for o, u in zip(own, above)]
    return interpolate(endogenous, index, weight, me)


def forward_half(
    a, own, above, drift, me, table_ref,
    index_ref, weight_ref, steady_ref, lottery_ref, target_ref, population_ref,
    mass_scr, row_scr, hot_ref=None,
):
    values = []
    for d in range(2):
        index = plane_of(index_ref, a, d)
        weight = plane_of(weight_ref, a, d)
        policy = policy_plane(own[d], above[d], drift, index, weight, me)
        values.append(GROSS_RATE / (policy * policy))
        share = plane_of(lottery_ref, a, d) + SLOPE_GAIN * (policy - plane_of(steady_ref, a, d))
        share = jnp.clip(share, 0.0, 1.0)
        population = plane_of(population_ref, a, d)
        rows = slice(d * Z, (d + 1) * Z)
        mass_scr[0, rows, :] = population * share
        mass_scr[1, rows, :] = population * (1.0 - share)

    sub8 = lax.broadcasted_iota(jnp.int32, (8, LANES), 0)
    is_low = sub8 < 4
    sub_quarter = sub8 & 3
    sub128 = lax.broadcasted_iota(jnp.int32, (LANES, LANES), 0)
    for d in range(2):
        for z in range(Z):
            row = d * Z + z
            target = target_ref[pl.ds(4 * z + 2 * d + a, 1), :]
            quarter = ((target >> 7) - me) & 3
            if hot_ref is None:
                hot, hot_lanes = jnp.where(sub128 == (target & 127), 1.0, 0.0).astype(jnp.bfloat16), 1
            else:
                hot, hot_lanes = hot_ref[row * LANES : (row + 1) * LANES, :], 0
            mass = jnp.where(is_low, mass_scr[0, row : row + 1, :], mass_scr[1, row : row + 1, :])
            mass = jnp.where(quarter == sub_quarter, mass, 0.0)
            first = mass.astype(jnp.bfloat16)
            rest = mass - first.astype(jnp.float32)
            both = jnp.concatenate([mass, rest], axis=0).astype(jnp.bfloat16)
            out = lax.dot_general(both, hot, (((1,), (hot_lanes,)), ((), ())), preferred_element_type=jnp.float32)
            row_scr[row * 8 : row * 8 + 8, :] = out[:8] + out[8:]
    scaled = table_ref[8:, :Z] * (DISCOUNT * GROSS_RATE)
    expected = split_lanes(dot_full(scaled, jnp.concatenate(values, axis=1)), 2)
    lane = lax.broadcasted_iota(jnp.int32, (HALF_ROWS, LANES), 1)
    low = [row_scr[pl.ds(q, HALF_ROWS, stride=8), :] for q in range(4)]
    high = [pltpu.roll(row_scr[pl.ds(4 + q, HALF_ROWS, stride=8), :], 1, 1) for q in range(4)]
    rows_by_quarter = [low[q] + jnp.where(lane == 0, high[(q + 3) % 4], high[q]) for q in range(4)]
    return expected, rows_by_quarter


def last_drift(drift_ref):
    is_last = lax.axis_index("ill") == lax.axis_size("ill") - 1
    return jnp.where(is_last, 1.0, drift_ref[1])


def stay_of(keep_ref):
    return jnp.where(lax.axis_index("dur") == 0, 1.0, keep_ref[0]), keep_ref[1]


def rows_of(refs, p):
    return [ref[p * Z : (p + 1) * Z, :] for ref in refs]


def rows_of(refs, p):
    return [ref[p * Z : (p + 1) * Z, :] for ref in refs]


def hot_kernel(target_ref, out_ref):
    lanes = lax.broadcasted_iota(jnp.int32, (LANES, LANES), 1)
    planes = [plane_of(target_ref, 1, d) & 127 for d in range(2)]
    turned_target = jnp.concatenate(planes + [jnp.zeros((HALF_ROWS, LANES), jnp.int32)], axis=0).T
    for row in range(HALF_ROWS):
        hot = jnp.where(lanes == turned_target[:, row : row + 1], 1.0, 0.0)
        out_ref[row * LANES : (row + 1) * LANES, :] = hot.astype(jnp.bfloat16)


def first_half_kernel(
    table_ref, v0, v1, v2, v3, index_ref, weight_ref, steady_ref, lottery_ref, target_ref,
    population_ref, mass_ref, expected_ref, upper_ref, mass_scr, row_scr,
):
    values = []
    for p in range(4):
        values += [v0[p * Z : (p + 1) * Z, :]] + [plane_of(ref, p // 2, p % 2) for ref in (v1, v2, v3)]
    planes = split_lanes(dot_full(table_ref[8:, :Z] * (table_ref[8:, Z : Z + 1] * (DISCOUNT * GROSS_RATE)), jnp.concatenate(values, axis=1)), 16)
    for i in range(8):
        upper_ref[i * Z : (i + 1) * Z, :] = planes[8 + i]
    expected, by_quarter = forward_half(
        0, [planes[0:4], planes[4:8]], [planes[8:12], planes[12:16]], table_ref[0:1, :],
        lax.axis_index("liq"), table_ref, index_ref, weight_ref, steady_ref, lottery_ref, target_ref,
        population_ref, mass_scr, row_scr,
    )
    for q in range(4):
        mass_ref[q * HALF_ROWS : (q + 1) * HALF_ROWS, :] = by_quarter[q]
    for d in range(2):
        expected_ref[d * Z : (d + 1) * Z, :] = expected[d]


def second_half_kernel(
    table_ref, upper_ref, halo_ref, first_ref, hot_ref, index_ref, weight_ref, steady_ref,
    lottery_ref, target_ref, population_ref, p0, p1, p2, p3, expected_ref, mass_scr, row_scr,
):
    own = [[upper_ref[(4 * d + q) * Z : (4 * d + q + 1) * Z, :] for q in range(4)] for d in range(2)]
    values = [halo_ref[q * HALF_ROWS + d * Z : q * HALF_ROWS + (d + 1) * Z, :] for d in range(2) for q in range(4)]
    planes = split_lanes(dot_full(table_ref[8:, :Z] * (table_ref[8:, Z : Z + 1] * (DISCOUNT * GROSS_RATE)), jnp.concatenate(values, axis=1)), 8)
    expected, by_quarter = forward_half(
        1, own, [planes[0:4], planes[4:8]], table_ref[1:2, :],
        lax.axis_index("liq"), table_ref, index_ref, weight_ref, steady_ref, lottery_ref, target_ref,
        population_ref, mass_scr, row_scr, hot_ref,
    )
    for q, out in enumerate((p0, p1, p2, p3)):
        out[:HALF_ROWS, :] = first_ref[q * HALF_ROWS : (q + 1) * HALF_ROWS, :]
        out[HALF_ROWS:, :] = by_quarter[q]
    for d in range(2):
        expected_ref[d * Z : (d + 1) * Z, :] = expected[d]


def consume_kernel(table_ref, e0, e1, e2, e3, index_ref, weight_ref, out_ref):
    pieces = (e0, e1, e2, e3)
    for a in range(2):
        for d in range(2):
            policy = policy_plane(
                rows_of(pieces, 2 * a + d), rows_of(pieces, 2 * a + 2 + d), table_ref[a : a + 1, :],
                plane_of(index_ref, a, d), plane_of(weight_ref, a, d), lax.axis_index("liq"),
            )
            out_ref[pl.ds(2 * d + a, Z, stride=4), :] = policy


def gather_mass_kernel(table_ref, p0, p1, p2, p3, lower_ref, upper_ref, halo_ref, core_out, expected_out):
    core_out[:PLANE_ROWS, :] = (p0[...] + p1[...]) + (p2[...] + p3[...])
    core_out[PLANE_ROWS:, :] = table_ref[:8, :]
    for i, ref in enumerate((lower_ref, upper_ref, halo_ref)):
        expected_out[i * HALF_ROWS : (i + 1) * HALF_ROWS, :] = ref[...]


def leave_kernel(own_ref, core_ref, dur_out):
    for i, ref in enumerate((own_ref, core_ref)):
        leave = 1.0 - ref[PLANE_ROWS + 2 : PLANE_ROWS + 3, :]
        for a in range(2):
            row = i * HALF_ROWS + a * Z
            dur_out[row : row + Z, :] = leave * ref[2 * a * Z : (2 * a + 1) * Z, :]
        dur_out[PLANE_ROWS + 8 * i : PLANE_ROWS + 8 * i + 8, :] = ref[PLANE_ROWS:, :]


def spread_targets(small):
    rows = lax.broadcasted_iota(jnp.int32, (Z, LANES), 0)
    lane = lax.broadcasted_iota(jnp.int32, (Z, LANES), 1)
    picked = [jnp.where(lane == rows, row, 0.0) for row in small]
    picked = jnp.concatenate(picked, axis=0).astype(jnp.bfloat16)
    ones = jnp.ones((LANES, LANES), jnp.bfloat16)
    return jnp.dot(picked, ones, preferred_element_type=jnp.float32)


def settle_kernel(own_ref, core_ref, dur_ref, o0, o1, o2, o3):
    sources = ([], [])
    for ref in (own_ref, core_ref):
        targets = spread_targets([ref[PLANE_ROWS + row : PLANE_ROWS + row + 1, :] for row in (4, 6, 5, 7)])
        for p in range(4):
            sources[p % 2].append((targets[p * Z : (p + 1) * Z], ref[p * Z : (p + 1) * Z, :]))
    arriving = []
    targets = spread_targets(
        [dur_ref[PLANE_ROWS + row : PLANE_ROWS + row + 1, :] for row in (4, 5, 12, 13)]
    )
    for i in range(4):
        arriving.append((targets[i * Z : (i + 1) * Z], dur_ref[i * Z : (i + 1) * Z, :]))
    ill = lax.axis_index("ill")
    y, core = ill >> 1, ill & 1
    stay_low, stay_high = own_ref[PLANE_ROWS + 2 : PLANE_ROWS + 3, :], own_ref[PLANE_ROWS + 3 : PLANE_ROWS + 4, :]
    leave_high = 1.0 - stay_high
    for k, out in enumerate((o0, o1, o2, o3)):
        for a in range(2):
            point = (4 * ((y + k) & 3) + 2 * core + a).astype(jnp.float32)

            def gathered(pairs):
                parts = [jnp.where(target == point, mass, 0.0) for target, mass in pairs]
                return (parts[0] + parts[1]) + (parts[2] + parts[3])

            low, high = gathered(sources[0]), gathered(sources[1])
            out[2 * a * Z : (2 * a + 1) * Z, :] = stay_low * low + leave_high * high
            out[(2 * a + 1) * Z : (2 * a + 2) * Z, :] = stay_high * high + gathered(arriving)


def population_kernel(table_ref, s0, s1, s2, s3, out_ref):
    settled = (s0[...] + s1[...]) + (s2[...] + s3[...])
    wide = jnp.concatenate([settled[p * Z : (p + 1) * Z] for p in range(4)], axis=1)
    moved = lax.dot_general(
        table_ref[8:, :Z], wide, (((0,), (0,)), ((), ())), precision=HIGHEST_PREC, preferred_element_type=jnp.float32
    )
    for p, plane in enumerate(split_lanes(moved, 4)):
        a, d = p // 2, p % 2
        out_ref[pl.ds(2 * d + a, Z, stride=4), :] = plane


def call(kernel, out_rows, inputs, scratch=(), work=0, dtype=jnp.float32, spaces=None):
    shapes = [jax.ShapeDtypeStruct((rows, LANES), dtype) for rows in out_rows]
    specs = [pl.BlockSpec(memory_space=VMEM) for _ in out_rows]
    single = len(out_rows) == 1
    return pl.pallas_call(
        kernel,
        out_shape=shapes[0] if single else shapes,
        in_specs=[pl.BlockSpec(memory_space=space) for space in spaces or [VMEM] * len(inputs)],
        out_specs=specs[0] if single else specs,
        scratch_shapes=list(scratch),
        compiler_params=pltpu.CompilerParams(vmem_limit_bytes=KERNEL_VMEM),
        cost_estimate=pl.CostEstimate(flops=0, transcendentals=0, bytes_accessed=work) if work else None,
    )(*inputs)


def turned(axis, distance):
    count = lax.axis_size(axis)
    return [(i, (i + distance) % count) for i in range(count)]


def from_other_liq(pieces):
    got = [lax.ppermute(pieces[k], "liq", turned("liq", k)) for k in range(1, 4)]
    return [got[3 - k] for k in range(1, 4)]


def from_above_ill(x):
    return lax.ppermute(x, "ill", turned("ill", -1))


def body(
    marginal_value, transition, discount_shock, illiquid_drift, durable_keep, bracket_index, bracket_weight,
    steady_consumption, lottery_weight, liquid_target, illiquid_target, population,
):
    flat = lambda x: x.reshape(PLANE_ROWS, LANES)
    ill_count, dur_count = lax.axis_size("ill"), lax.axis_size("dur")
    index, weight = flat(bracket_index), flat(bracket_weight)
    states = [index, weight] + [flat(x) for x in (steady_consumption, lottery_weight, liquid_target, population)]
    scratch = [pltpu.VMEM((2, HALF_ROWS, LANES), jnp.float32), pltpu.VMEM((8 * HALF_ROWS, LANES), jnp.float32)]
    below_dur = [(d, d - 1) for d in range(1, dur_count)]
    other_core = [(i, i ^ 1) for i in range(ill_count)]

    with jax.named_scope("value_over_liq"):
        value = flat(marginal_value)
        pieces = [marginal_value.transpose(2, 1, 0, 3).reshape(PLANE_ROWS, LANES)] + from_other_liq([value] * 4)
    with jax.named_scope("prepare"):
        is_last = lax.axis_index("ill") == ill_count - 1
        is_lowest = lax.axis_index("dur") == 0
        row = lax.broadcasted_iota(jnp.int32, (2, LANES), 0)
        drift = jnp.where((row == 1) & is_last, 1.0, illiquid_drift[:, None])
        stay = jnp.where((row == 0) & is_lowest, 1.0, durable_keep[:, None])
        target = illiquid_target.transpose(1, 2, 0).reshape(4, Z).astype(jnp.float32)
        target = jnp.pad(target, ((0, 0), (0, LANES - Z)))
        income = jnp.concatenate(
            [transition, discount_shock[:, None], jnp.zeros((Z, LANES - Z - 1), jnp.float32)], axis=1
        )
        table = jnp.concatenate([drift, stay, target, income], axis=0)
    with jax.named_scope("hot"):
        hot = call(hot_kernel, [HALF_ROWS * LANES], [flat(liquid_target)], dtype=jnp.bfloat16)
    with jax.named_scope("value_over_ill"):
        halo = from_above_ill(call(pack_kernel, [4 * HALF_ROWS], [*pieces, hot], spaces=[VMEM] * 4 + [pl.ANY]))
    with jax.named_scope("first_half"):
        mass, lower, upper = call(
            first_half_kernel,
            [4 * HALF_ROWS, HALF_ROWS, 4 * HALF_ROWS],
            [table, *pieces, *states],
            scratch,
        )
    with jax.named_scope("expected_over_ill"):
        next_halo = from_above_ill(lower)
    with jax.named_scope("second_half"):
        *sends, higher = call(
            second_half_kernel,
            [PLANE_ROWS] * 4 + [HALF_ROWS],
            [table, upper, halo, mass, hot, *states],
            scratch,
            30000000,
        )
    with jax.named_scope("mass_over_liq"):
        got = [sends[0]] + from_other_liq(sends)
    with jax.named_scope("gather_mass"):
        to_core, expected = call(
            gather_mass_kernel, [PLANE_ROWS + 8, 3 * HALF_ROWS], [table, *got, lower, higher, next_halo]
        )
    with jax.named_scope("mass_over_core"):
        from_core = lax.ppermute(to_core, "ill", other_core)
    with jax.named_scope("leave"):
        to_dur = call(leave_kernel, [PLANE_ROWS + 16], [to_core, from_core])
    with jax.named_scope("mass_over_dur"):
        from_dur = lax.ppermute(to_dur, "dur", below_dur)
    with jax.named_scope("expected_over_liq"):
        expected_pieces = [expected] + from_other_liq([expected] * 4)
    with jax.named_scope("settle"):
        parts = call(settle_kernel, [PLANE_ROWS] * 4, [to_core, from_core, from_dur])
    with jax.named_scope("mass_over_ill"):
        arrived = [lax.ppermute(parts[k], "ill", turned("ill", 2 * k)) for k in range(1, 4)]
    with jax.named_scope("consume"):
        consumption = call(consume_kernel, [PLANE_ROWS], [table, *expected_pieces, index, weight])
    with jax.named_scope("population"):
        population_next = call(population_kernel, [PLANE_ROWS], [table, parts[0], *arrived])
    shape = population.shape
    return consumption.reshape(shape), population_next.reshape(shape)


def solution(mesh):
    state = P(None, "dur", "ill", "liq")
    in_specs = (
        state, P(), P(), P("ill"), P("dur"), state, state, state, state, state, P(None, "dur", "ill"), state,
    )
    return jax.shard_map(body, mesh=mesh, in_specs=in_specs, out_specs=(state, state), check_vma=False)
```

```python
import functools

import jax
import jax.numpy as jnp
from jax import lax
from jax.experimental import pallas as pl
from jax.experimental.pallas import tpu as pltpu
from jax.sharding import PartitionSpec as P

DISCOUNT = 0.96
GROSS_RATE = 1.01
SLOPE_GAIN = 0.5
HIGHEST_PREC = lax.Precision.HIGHEST

Z = 32
LANES = 128
PLANE_ROWS = 4 * Z
HALF_ROWS = 2 * Z
KERNEL_VMEM = 4 << 20
VMEM = pltpu.VMEM
SMEM = pltpu.SMEM


def plane_of(ref, a, d):
    return ref[pl.ds(2 * d + a, Z, stride=4), :]


def dot_full(left, right):
    return jnp.dot(left, right, precision=HIGHEST_PREC, preferred_element_type=jnp.float32)


def split_lanes(wide, count):
    return [wide[:, i * LANES : (i + 1) * LANES] for i in range(count)]


def pack_kernel(v0, v1, v2, v3, hot_ref, out_ref):
    del hot_ref
    for q, ref in enumerate((v1, v2, v3)):
        for d in range(2):
            out_ref[(q + 1) * HALF_ROWS + d * Z : (q + 1) * HALF_ROWS + (d + 1) * Z, :] = plane_of(ref, 0, d)
    out_ref[:HALF_ROWS, :] = v0[:HALF_ROWS, :]


def interpolate(pieces, index, weight, me):
    upper_index = index + 1
    quarter = ((index >> 7) - me) & 3
    upper_quarter = ((upper_index >> 7) - me) & 3
    lane = index & 127
    upper_lane = upper_index & 127
    lower = upper = None
    for q, piece in enumerate(pieces):
        low = jnp.take_along_axis(piece, lane, axis=1, mode="promise_in_bounds")
        high = jnp.take_along_axis(piece, upper_lane, axis=1, mode="promise_in_bounds")
        lower = low if lower is None else jnp.where(quarter == q, low, lower)
        upper = high if upper is None else jnp.where(upper_quarter == q, high, upper)
    return weight * lower + (1.0 - weight) * upper


def policy_plane(own, above, drift, index, weight, me):
    endogenous = [lax.rsqrt(drift * o + (1.0 - drift) * u) for o, u in zip(own, above)]
    return interpolate(endogenous, index, weight, me)


def forward_half(
    a, own, above, drift, me, table_ref,
    index_ref, weight_ref, steady_ref, lottery_ref, target_ref, population_ref,
    mass_scr, row_scr, hot_ref=None,
):
    values = []
    for d in range(2):
        index = plane_of(index_ref, a, d)
        weight = plane_of(weight_ref, a, d)
        policy = policy_plane(own[d], above[d], drift, index, weight, me)
        values.append(GROSS_RATE / (policy * policy))
        share = plane_of(lottery_ref, a, d) + SLOPE_GAIN * (policy - plane_of(steady_ref, a, d))
        share = jnp.clip(share, 0.0, 1.0)
        population = plane_of(population_ref, a, d)
        rows = slice(d * Z, (d + 1) * Z)
        mass_scr[0, rows, :] = population * share
        mass_scr[1, rows, :] = population * (1.0 - share)

    sub8 = lax.broadcasted_iota(jnp.int32, (8, LANES), 0)
    is_low = sub8 < 4
    sub_quarter = sub8 & 3
    sub128 = lax.broadcasted_iota(jnp.int32, (LANES, LANES), 0)
    for d in range(2):
        for z in range(Z):
            row = d * Z + z
            target = target_ref[pl.ds(4 * z + 2 * d + a, 1), :]
            quarter = ((target >> 7) - me) & 3
            if hot_ref is None:
                hot, hot_lanes = jnp.where(sub128 == (target & 127), 1.0, 0.0).astype(jnp.bfloat16), 1
            else:
                hot, hot_lanes = hot_ref[row * LANES : (row + 1) * LANES, :], 0
            mass = jnp.where(is_low, mass_scr[0, row : row + 1, :], mass_scr[1, row : row + 1, :])
            mass = jnp.where(quarter == sub_quarter, mass, 0.0)
            first = mass.astype(jnp.bfloat16)
            rest = mass - first.astype(jnp.float32)
            both = jnp.concatenate([mass, rest], axis=0).astype(jnp.bfloat16)
            out = lax.dot_general(both, hot, (((1,), (hot_lanes,)), ((), ())), preferred_element_type=jnp.float32)
            row_scr[row * 8 : row * 8 + 8, :] = out[:8] + out[8:]
    scaled = table_ref[8:, :Z] * (DISCOUNT * GROSS_RATE)
    expected = split_lanes(dot_full(scaled, jnp.concatenate(values, axis=1)), 2)
    lane = lax.broadcasted_iota(jnp.int32, (HALF_ROWS, LANES), 1)
    low = [row_scr[pl.ds(q, HALF_ROWS, stride=8), :] for q in range(4)]
    high = [pltpu.roll(row_scr[pl.ds(4 + q, HALF_ROWS, stride=8), :], 1, 1) for q in range(4)]
    rows_by_quarter = [low[q] + jnp.where(lane == 0, high[(q + 3) % 4], high[q]) for q in range(4)]
    return expected, rows_by_quarter


def last_drift(drift_ref):
    is_last = lax.axis_index("ill") == lax.axis_size("ill") - 1
    return jnp.where(is_last, 1.0, drift_ref[1])


def stay_of(keep_ref):
    return jnp.where(lax.axis_index("dur") == 0, 1.0, keep_ref[0]), keep_ref[1]


def rows_of(refs, p):
    return [ref[p * Z : (p + 1) * Z, :] for ref in refs]


def rows_of(refs, p):
    return [ref[p * Z : (p + 1) * Z, :] for ref in refs]


def hot_kernel(target_ref, out_ref):
    lanes = lax.broadcasted_iota(jnp.int32, (LANES, LANES), 1)
    planes = [plane_of(target_ref, 1, d) & 127 for d in range(2)]
    turned_target = jnp.concatenate(planes + [jnp.zeros((HALF_ROWS, LANES), jnp.int32)], axis=0).T
    for row in range(HALF_ROWS):
        hot = jnp.where(lanes == turned_target[:, row : row + 1], 1.0, 0.0)
        out_ref[row * LANES : (row + 1) * LANES, :] = hot.astype(jnp.bfloat16)


def first_half_kernel(
    table_ref, v0, v1, v2, v3, index_ref, weight_ref, steady_ref, lottery_ref, target_ref,
    population_ref, mass_ref, expected_ref, upper_ref, mass_scr, row_scr,
):
    values = []
    for p in range(4):
        values += [v0[p * Z : (p + 1) * Z, :]] + [plane_of(ref, p // 2, p % 2) for ref in (v1, v2, v3)]
    planes = split_lanes(dot_full(table_ref[8:, :Z] * (table_ref[8:, Z : Z + 1] * (DISCOUNT * GROSS_RATE)), jnp.concatenate(values, axis=1)), 16)
    for i in range(8):
        upper_ref[i * Z : (i + 1) * Z, :] = planes[8 + i]
    expected, by_quarter = forward_half(
        0, [planes[0:4], planes[4:8]], [planes[8:12], planes[12:16]], table_ref[0:1, :],
        lax.axis_index("liq"), table_ref, index_ref, weight_ref, steady_ref, lottery_ref, target_ref,
        population_ref, mass_scr, row_scr,
    )
    for q in range(4):
        mass_ref[q * HALF_ROWS : (q + 1) * HALF_ROWS, :] = by_quarter[q]
    for d in range(2):
        expected_ref[d * Z : (d + 1) * Z, :] = expected[d]


def second_half_kernel(
    table_ref, upper_ref, halo_ref, first_ref, hot_ref, index_ref, weight_ref, steady_ref,
    lottery_ref, target_ref, population_ref, p0, p1, p2, p3, expected_ref, mass_scr, row_scr,
):
    own = [[upper_ref[(4 * d + q) * Z : (4 * d + q + 1) * Z, :] for q in range(4)] for d in range(2)]
    values = [halo_ref[q * HALF_ROWS + d * Z : q * HALF_ROWS + (d + 1) * Z, :] for d in range(2) for q in range(4)]
    planes = split_lanes(dot_full(table_ref[8:, :Z] * (table_ref[8:, Z : Z + 1] * (DISCOUNT * GROSS_RATE)), jnp.concatenate(values, axis=1)), 8)
    expected, by_quarter = forward_half(
        1, own, [planes[0:4], planes[4:8]], table_ref[1:2, :],
        lax.axis_index("liq"), table_ref, index_ref, weight_ref, steady_ref, lottery_ref, target_ref,
        population_ref, mass_scr, row_scr, hot_ref,
    )
    for q, out in enumerate((p0, p1, p2, p3)):
        out[:HALF_ROWS, :] = first_ref[q * HALF_ROWS : (q + 1) * HALF_ROWS, :]
        out[HALF_ROWS:, :] = by_quarter[q]
    for d in range(2):
        expected_ref[d * Z : (d + 1) * Z, :] = expected[d]


def consume_kernel(table_ref, e0, e2, e1, e3, index_ref, weight_ref, out_ref):
    pieces = (e0, e1, e2, e3)
    for a in range(2):
        for d in range(2):
            policy = policy_plane(
                rows_of(pieces, 2 * a + d), rows_of(pieces, 2 * a + 2 + d), table_ref[a : a + 1, :],
                plane_of(index_ref, a, d), plane_of(weight_ref, a, d), lax.axis_index("liq"),
            )
            out_ref[pl.ds(2 * d + a, Z, stride=4), :] = policy


def gather_mass_kernel(table_ref, p0, p1, p2, p3, lower_ref, upper_ref, halo_ref, core_out, expected_out):
    core_out[:PLANE_ROWS, :] = (p0[...] + p1[...]) + (p2[...] + p3[...])
    core_out[PLANE_ROWS:, :] = table_ref[:8, :]
    for i, ref in enumerate((lower_ref, upper_ref, halo_ref)):
        expected_out[i * HALF_ROWS : (i + 1) * HALF_ROWS, :] = ref[...]


def leave_kernel(own_ref, core_ref, dur_out):
    for i, ref in enumerate((own_ref, core_ref)):
        leave = 1.0 - ref[PLANE_ROWS + 2 : PLANE_ROWS + 3, :]
        for a in range(2):
            row = i * HALF_ROWS + a * Z
            dur_out[row : row + Z, :] = leave * ref[2 * a * Z : (2 * a + 1) * Z, :]
        dur_out[PLANE_ROWS + 8 * i : PLANE_ROWS + 8 * i + 8, :] = ref[PLANE_ROWS:, :]


def spread_targets(small):
    rows = lax.broadcasted_iota(jnp.int32, (Z, LANES), 0)
    lane = lax.broadcasted_iota(jnp.int32, (Z, LANES), 1)
    picked = [jnp.where(lane == rows, row, 0.0) for row in small]
    picked = jnp.concatenate(picked, axis=0).astype(jnp.bfloat16)
    ones = jnp.ones((LANES, LANES), jnp.bfloat16)
    return jnp.dot(picked, ones, preferred_element_type=jnp.float32)


def settle_kernel(own_ref, core_ref, dur_ref, o0, o1, o2, o3):
    sources = ([], [])
    for ref in (own_ref, core_ref):
        targets = spread_targets([ref[PLANE_ROWS + row : PLANE_ROWS + row + 1, :] for row in (4, 6, 5, 7)])
        for p in range(4):
            sources[p % 2].append((targets[p * Z : (p + 1) * Z], ref[p * Z : (p + 1) * Z, :]))
    arriving = []
    targets = spread_targets(
        [dur_ref[PLANE_ROWS + row : PLANE_ROWS + row + 1, :] for row in (4, 5, 12, 13)]
    )
    for i in range(4):
        arriving.append((targets[i * Z : (i + 1) * Z], dur_ref[i * Z : (i + 1) * Z, :]))
    ill = lax.axis_index("ill")
    y, core = ill >> 1, ill & 1
    stay_low, stay_high = own_ref[PLANE_ROWS + 2 : PLANE_ROWS + 3, :], own_ref[PLANE_ROWS + 3 : PLANE_ROWS + 4, :]
    leave_high = 1.0 - stay_high
    for k, out in enumerate((o0, o1, o2, o3)):
        for a in range(2):
            point = (4 * ((y + k) & 3) + 2 * core + a).astype(jnp.float32)

            def gathered(pairs):
                parts = [jnp.where(target == point, mass, 0.0) for target, mass in pairs]
                return (parts[0] + parts[1]) + (parts[2] + parts[3])

            low, high = gathered(sources[0]), gathered(sources[1])
            out[2 * a * Z : (2 * a + 1) * Z, :] = stay_low * low + leave_high * high
            out[(2 * a + 1) * Z : (2 * a + 2) * Z, :] = stay_high * high + gathered(arriving)


def population_kernel(table_ref, s0, s1, s2, s3, out_ref):
    settled = (s0[...] + s1[...]) + (s2[...] + s3[...])
    wide = jnp.concatenate([settled[p * Z : (p + 1) * Z] for p in range(4)], axis=1)
    moved = lax.dot_general(
        table_ref[8:, :Z], wide, (((0,), (0,)), ((), ())), precision=HIGHEST_PREC, preferred_element_type=jnp.float32
    )
    for p, plane in enumerate(split_lanes(moved, 4)):
        a, d = p // 2, p % 2
        out_ref[pl.ds(2 * d + a, Z, stride=4), :] = plane


def call(kernel, out_rows, inputs, scratch=(), work=0, dtype=jnp.float32, spaces=None):
    shapes = [jax.ShapeDtypeStruct((rows, LANES), dtype) for rows in out_rows]
    specs = [pl.BlockSpec(memory_space=VMEM) for _ in out_rows]
    single = len(out_rows) == 1
    return pl.pallas_call(
        kernel,
        out_shape=shapes[0] if single else shapes,
        in_specs=[pl.BlockSpec(memory_space=space) for space in spaces or [VMEM] * len(inputs)],
        out_specs=specs[0] if single else specs,
        scratch_shapes=list(scratch),
        compiler_params=pltpu.CompilerParams(vmem_limit_bytes=KERNEL_VMEM),
        cost_estimate=pl.CostEstimate(flops=0, transcendentals=0, bytes_accessed=work) if work else None,
    )(*inputs)


def turned(axis, distance):
    count = lax.axis_size(axis)
    return [(i, (i + distance) % count) for i in range(count)]


def from_other_liq(pieces):
    got = [lax.ppermute(pieces[k], "liq", turned("liq", k)) for k in range(1, 4)]
    return [got[3 - k] for k in range(1, 4)]


def from_above_ill(x):
    return lax.ppermute(x, "ill", turned("ill", -1))


def body(
    marginal_value, transition, discount_shock, illiquid_drift, durable_keep, bracket_index, bracket_weight,
    steady_consumption, lottery_weight, liquid_target, illiquid_target, population,
):
    flat = lambda x: x.reshape(PLANE_ROWS, LANES)
    ill_count, dur_count = lax.axis_size("ill"), lax.axis_size("dur")
    index, weight = flat(bracket_index), flat(bracket_weight)
    states = [index, weight] + [flat(x) for x in (steady_consumption, lottery_weight, liquid_target, population)]
    scratch = [pltpu.VMEM((2, HALF_ROWS, LANES), jnp.float32), pltpu.VMEM((8 * HALF_ROWS, LANES), jnp.float32)]
    below_dur = [(d, d - 1) for d in range(1, dur_count)]
    other_core = [(i, i ^ 1) for i in range(ill_count)]

    with jax.named_scope("value_over_liq"):
        value = flat(marginal_value)
        pieces = [marginal_value.transpose(2, 1, 0, 3).reshape(PLANE_ROWS, LANES)] + from_other_liq([value] * 4)
    with jax.named_scope("prepare"):
        is_last = lax.axis_index("ill") == ill_count - 1
        is_lowest = lax.axis_index("dur") == 0
        row = lax.broadcasted_iota(jnp.int32, (2, LANES), 0)
        drift = jnp.where((row == 1) & is_last, 1.0, illiquid_drift[:, None])
        stay = jnp.where((row == 0) & is_lowest, 1.0, durable_keep[:, None])
        target = illiquid_target.transpose(1, 2, 0).reshape(4, Z).astype(jnp.float32)
        target = jnp.pad(target, ((0, 0), (0, LANES - Z)))
        income = jnp.concatenate(
            [transition, discount_shock[:, None], jnp.zeros((Z, LANES - Z - 1), jnp.float32)], axis=1
        )
        table = jnp.concatenate([drift, stay, target, income], axis=0)
    with jax.named_scope("hot"):
        hot = call(hot_kernel, [HALF_ROWS * LANES], [flat(liquid_target)], dtype=jnp.bfloat16)
    with jax.named_scope("value_over_ill"):
        halo = from_above_ill(call(pack_kernel, [4 * HALF_ROWS], [*pieces, hot], spaces=[VMEM] * 4 + [pl.ANY]))
    with jax.named_scope("first_half"):
        mass, lower, upper = call(
            first_half_kernel,
            [4 * HALF_ROWS, HALF_ROWS, 4 * HALF_ROWS],
            [table, *pieces, *states],
            scratch,
        )
    with jax.named_scope("expected_over_ill"):
        next_halo = from_above_ill(lower)
    with jax.named_scope("second_half"):
        *sends, higher = call(
            second_half_kernel,
            [PLANE_ROWS] * 4 + [HALF_ROWS],
            [table, upper, halo, mass, hot, *states],
            scratch,
            30000000,
        )
    with jax.named_scope("mass_over_liq"):
        got = [sends[0]] + from_other_liq(sends)
    with jax.named_scope("gather_mass"):
        to_core, expected = call(
            gather_mass_kernel, [PLANE_ROWS + 8, 3 * HALF_ROWS], [table, *got, lower, higher, next_halo]
        )
    with jax.named_scope("mass_over_core"):
        from_core = lax.ppermute(to_core, "ill", other_core)
    with jax.named_scope("leave"):
        to_dur = call(leave_kernel, [PLANE_ROWS + 16], [to_core, from_core])
    with jax.named_scope("mass_over_dur"):
        from_dur = lax.ppermute(to_dur, "dur", below_dur)
    with jax.named_scope("expected_over_liq"):
        expected_pieces = [expected] + from_other_liq([expected] * 4)
    with jax.named_scope("settle"):
        parts = call(settle_kernel, [PLANE_ROWS] * 4, [to_core, from_core, from_dur])
    with jax.named_scope("mass_over_ill"):
        arrived = [lax.ppermute(parts[k], "ill", turned("ill", 2 * k)) for k in range(1, 4)]
    with jax.named_scope("consume"):
        consumption = call(consume_kernel, [PLANE_ROWS], [table, *(expected_pieces[q] for q in (0, 2, 1, 3)), index, weight])
    with jax.named_scope("population"):
        population_next = call(population_kernel, [PLANE_ROWS], [table, parts[0], *arrived])
    shape = population.shape
    return consumption.reshape(shape), population_next.reshape(shape)


def solution(mesh):
    state = P(None, "dur", "ill", "liq")
    in_specs = (
        state, P(), P(), P("ill"), P("dur"), state, state, state, state, state, P(None, "dur", "ill"), state,
    )
    return jax.shard_map(body, mesh=mesh, in_specs=in_specs, out_specs=(state, state), check_vma=False)
```
